1024 devices in a mesh: dp: 64 (over x, y, core), mp: 16 (over z).
Axes of the slice: x: 4, y: 8, z: 16, core: 2. Of those that a mesh axis runs over, the one named last changes fastest.
Arguments:
- query_rows: bfloat16 [16384, 6144], P('dp', 'mp'), may hold values from -6 to 6
- key_rows: bfloat16 [16384, 6144], P('dp', 'mp'), may hold values from -6 to 6
- value_rows: bfloat16 [16384, 6144], P('dp', 'mp'), may hold values from -6 to 6
- proj_weight: bfloat16 [6144, 6144], P('mp'), may hold values from -0.078125 to 0.078125
- out_grad: bfloat16 [16384, 6144], P('dp', 'mp'), may hold values from -6 to 6
- image_starts: int32 [64, 256], replicated, may hold values from -1 to 128, as said below
Outputs:
- projected: bfloat16 [16384, 6144], P('dp', 'mp')
- grad_query: bfloat16 [16384, 6144], P('dp', 'mp')
- grad_key: bfloat16 [16384, 6144], P('dp', 'mp')
- grad_value: bfloat16 [16384, 6144], P('dp', 'mp')
The draws below stay inside these ranges and needn't reach their ends.
Inputs may be any that keep to these rules, and one draw needn't show every extreme that they name: `image_starts`: each used row holds the index, within its pack, of the first row of its image; unused rows hold -1. A pack's used rows come first without gaps and its images are contiguous. Images begin only at rows 0, 64 and 128; one at 64 only in packs that use more than 128 rows. The data loader fills packs two at a time, splitting one batch of images between them, so packs t and t + 32 form a pair: one of them uses all of its first 128 rows, has an image beginning at row 128 that runs to its last used row, and uses some rows past it; the other uses fewer than 128 rows; together they use exactly 256 rows.
All inputs are finite; a program needn't handle non-finite values.
Results may differ from the reference program's by a relative error of at most 0.022.
Values may be sent and summed in bfloat16 or wider, within the bound.
No kernel may reach another device: no remote copies, remote signals or barrier semaphores. Data moves between devices by JAX's collectives and lax.ppermute only.
A program may use at most 32 MiB of HBM per device.

```python
import math
import jax
import jax.numpy as jnp
from jax import lax

HEADS = 48
HEAD_DIM = 128
D = 6144
HEADS_DEV = 3
WORK_ROWS = 128
PACK_ROWS = 256
TOKENS = 16384
N_DP = 64
N_MP = 16


def pack_starts(key):
    key = jax.random.fold_in(key, 101)
    first_key, second_key, third_key = jax.random.split(key, 3)
    half_count = N_DP // 2
    heavy_lower = jax.random.randint(first_key, (half_count,), 0, 2)
    light_count = jax.random.randint(second_key, (half_count,), WORK_ROWS // 4, 3 * WORK_ROWS // 4 + 1)
    heavy_count = 2 * WORK_ROWS - light_count
    lower_count = jnp.where(heavy_lower == 1, heavy_count, light_count)
    upper_count = jnp.where(heavy_lower == 1, light_count, heavy_count)
    used_count = jnp.concatenate([lower_count, upper_count])
    positions = jnp.arange(PACK_ROWS, dtype=jnp.int32)
    middle_coin = jax.random.randint(third_key, (N_DP,), 0, 2) == 1
    middle_flags = (middle_coin & (used_count > WORK_ROWS))[:, None] & (positions[None, :] == WORK_ROWS // 2)
    boundary_flags = middle_flags | (positions[None, :] == 0) | (positions[None, :] == WORK_ROWS)
    boundary_marks = jnp.where(boundary_flags, positions[None, :], -1)
    running_starts = lax.cummax(boundary_marks, axis=1)
    return jnp.where(positions[None, :] < used_count[:, None], running_starts, -1).astype(jnp.int32)


def draw_image_starts(key, part):
    return pack_starts(key)


def draw_query_rows(key, part):
    key = jax.random.fold_in(key, 5)
    first_key = jax.random.fold_in(key, 0)
    samples = jax.random.truncated_normal(first_key, -6.0, 6.0, (TOKENS, HEADS, HEAD_DIM), jnp.float32)
    return samples.reshape(TOKENS, HEADS * HEAD_DIM).astype(jnp.bfloat16)


def draw_key_rows(key, part):
    key = jax.random.fold_in(key, 7)
    first_key = jax.random.fold_in(key, 0)
    samples = jax.random.truncated_normal(first_key, -6.0, 6.0, (TOKENS, HEADS, HEAD_DIM), jnp.float32)
    return samples.reshape(TOKENS, HEADS * HEAD_DIM).astype(jnp.bfloat16)


def block_scale(rng, extent, cuts, low, largest):
    level, own = 1.0, jax.random.fold_in(rng, 6)
    for axis_at, blocks in cuts:
        draws = jnp.exp(jax.random.uniform(jax.random.fold_in(own, axis_at), (blocks,), jnp.float32, low / len(cuts), largest / len(cuts)))
        level = level * jnp.repeat(draws, extent[axis_at] // blocks).reshape([-1 if axis == axis_at else 1 for axis in range(len(extent))])
    return level


def gaussian(key, extent, deviation, reach, pieces=(), held_as=jnp.bfloat16):
    values = deviation * jax.random.normal(key, extent, jnp.float32)
    if pieces:
        values = values * block_scale(key, extent, pieces, -0.22, 0.18)
    return jnp.clip(values, -reach, reach).astype(held_as)


def setup_inputs(seed: int = 0) -> dict:
    keys = jax.random.split(jax.random.key(seed), 7)
    query_rows = draw_query_rows(jax.random.fold_in(keys[6], 71), 0)
    key_rows = draw_key_rows(jax.random.fold_in(keys[6], 71), 0)
    value_rows = gaussian(keys[2], (TOKENS, D), 1.0, 6.0, ((0, 64), (1, 16)))
    proj_weight = gaussian(keys[3], (D, D), D ** -0.5, 0.078125, ((0, 16),))
    out_grad = gaussian(keys[4], (TOKENS, D), 1.0, 6.0, ((0, 64), (1, 16)))
    image_starts = draw_image_starts(jax.random.fold_in(keys[6], 71), 0)
    return {"query_rows": query_rows, "key_rows": key_rows, "value_rows": value_rows, "proj_weight": proj_weight, "out_grad": out_grad, "image_starts": image_starts}


def pack_forward_backward(inputs, proj_weight):
    query_rows, key_rows, value_rows, out_grad, starts = inputs
    root_dim = math.sqrt(HEAD_DIM)
    query_heads = query_rows.astype(jnp.float32).reshape(PACK_ROWS, HEADS, HEAD_DIM)
    key_heads = key_rows.astype(jnp.float32).reshape(PACK_ROWS, HEADS, HEAD_DIM)
    value_heads = value_rows.astype(jnp.float32).reshape(PACK_ROWS, HEADS, HEAD_DIM)
    same_image = starts[:, None] == starts[None, :]
    valid_rows = (starts >= 0)[:, None]
    scores = jnp.einsum('qhd,khd->hqk', query_heads, key_heads) / root_dim
    scores = jnp.where(same_image[None], scores, -jnp.inf)
    maxima = lax.optimization_barrier(jnp.max(scores, axis=2, keepdims=True))
    weights = jnp.exp(scores - maxima)
    probabilities = weights / lax.optimization_barrier(jnp.sum(weights, axis=2, keepdims=True))
    rounded = lax.optimization_barrier(probabilities.astype(jnp.bfloat16)).astype(jnp.float32)
    attended = jnp.einsum('hqk,khd->qhd', rounded, value_heads).reshape(PACK_ROWS, D)
    attended = jnp.where(valid_rows, attended, 0.0).astype(jnp.bfloat16)
    grouped = attended.astype(jnp.float32).reshape(PACK_ROWS, N_MP, HEADS_DEV * HEAD_DIM)
    weight_groups = proj_weight.astype(jnp.float32).reshape(N_MP, HEADS_DEV * HEAD_DIM, D)
    partials = jnp.einsum('tgc,gcd->gtd', grouped, weight_groups)
    partials = lax.optimization_barrier(partials.astype(jnp.bfloat16)).astype(jnp.float32)
    projected = lax.optimization_barrier(jnp.sum(partials, axis=0)).astype(jnp.bfloat16)
    grad_attended = lax.dot_general(out_grad, proj_weight, (((1,), (1,)), ((), ())), preferred_element_type=jnp.float32).astype(jnp.bfloat16)
    grad_heads = grad_attended.astype(jnp.float32).reshape(PACK_ROWS, HEADS, HEAD_DIM)
    grad_value = jnp.einsum('hqk,qhd->khd', rounded, grad_heads)
    grad_weights = jnp.einsum('qhd,khd->hqk', grad_heads, value_heads)
    correction = lax.optimization_barrier(jnp.sum(probabilities * grad_weights, axis=2, keepdims=True))
    grad_scores = probabilities * (grad_weights - correction) / root_dim
    grad_scores = lax.optimization_barrier(grad_scores.astype(jnp.bfloat16)).astype(jnp.float32)
    grad_query = jnp.einsum('hqk,khd->qhd', grad_scores, key_heads)
    grad_key = jnp.einsum('hqk,qhd->khd', grad_scores, query_heads)

    def finish(gradient):
        return jnp.where(valid_rows, gradient.reshape(PACK_ROWS, D), 0.0).astype(jnp.bfloat16)
    return (projected, finish(grad_query), finish(grad_key), finish(grad_value))

def reference(query_rows, key_rows, value_rows, proj_weight, out_grad, image_starts):

    def per_pack(inputs):
        return pack_forward_backward(inputs, proj_weight)
    packed = (query_rows.reshape(N_DP, PACK_ROWS, D), key_rows.reshape(N_DP, PACK_ROWS, D), value_rows.reshape(N_DP, PACK_ROWS, D), out_grad.reshape(N_DP, PACK_ROWS, D), image_starts)
    projected, grad_query, grad_key, grad_value = lax.map(per_pack, packed)
    return (projected.reshape(TOKENS, D), grad_query.reshape(TOKENS, D), grad_key.reshape(TOKENS, D), grad_value.reshape(TOKENS, D))
```

```python
import math

import jax
import jax.numpy as jnp
from jax import lax
from jax.sharding import PartitionSpec as P

HEAD_DIM = 128
SLOT = 128


def ring_pairs(dp_size, mp_size):
    pairs = []
    for dp in range(dp_size):
        step = 1 if goes_right(dp, dp_size) else mp_size - 1
        for z in range(mp_size):
            pairs.append((dp * mp_size + z, dp * mp_size + (z + step) % mp_size))
    return pairs


def goes_right(dp, dp_size):
    return (dp // (dp_size // 2) + dp) % 2 == 0


def dot(a, b, dims=(((1,), (0,)), ((), ()))):
    return lax.dot_general(a, b, dims, preferred_element_type=jnp.float32)


def shards(query_rows, key_rows, value_rows, proj_weight, out_grad, image_starts):
    dp_size, mp_size = lax.axis_size("dp"), lax.axis_size("mp")
    half_ring = mp_size // 2
    dp, z = lax.axis_index("dp"), lax.axis_index("mp")
    ring_perm = ring_pairs(dp_size, mp_size)
    swap_perm = [(i, (i + dp_size // 2) % dp_size) for i in range(dp_size)]
    right = goes_right(dp, dp_size)
    delta = jnp.where(right, 1, mp_size - 1)
    starts = lax.dynamic_index_in_dim(image_starts, dp, 0, keepdims=False)
    other_starts = lax.dynamic_index_in_dim(
        image_starts, (dp + dp_size // 2) % dp_size, 0, keepdims=False
    )
    heavy = starts[SLOT - 1] >= 0
    light_count = jnp.sum((jnp.where(heavy, other_starts, starts) >= 0).astype(jnp.int32))
    from_light = (jnp.arange(SLOT) < light_count)[:, None]
    flip = (jnp.arange(SLOT)[:, None] + jnp.arange(SLOT)[None, :] == SLOT - 1).astype(jnp.bfloat16)

    def ring(rows):
        return lax.ppermute(rows, ("dp", "mp"), ring_perm)

    def swap(rows):
        return lax.ppermute(rows, "dp", swap_perm)

    def pack(own, other):
        heavy_rows = jnp.where(heavy, own, other)
        light_rows = jnp.where(heavy, other[:SLOT], own[:SLOT])
        flipped = dot(flip, heavy_rows[SLOT:]).astype(jnp.bfloat16)
        return jnp.concatenate([heavy_rows[:SLOT], jnp.where(from_light, light_rows, flipped)], 0)

    def unpack(rows):
        first = jnp.where(heavy, rows[:SLOT], rows[SLOT:])
        return jnp.concatenate([first, dot(flip, rows[SLOT:]).astype(jnp.bfloat16)], 0)

    def half_of(rows):
        return jnp.where(right, rows[:SLOT], rows[SLOT:])

    def place_half(rows):
        zeros = jnp.zeros_like(rows)
        return jnp.concatenate([jnp.where(right, rows, zeros), jnp.where(right, zeros, rows)], 0)

    width = query_rows.shape[1]

    def weight_block(index):
        return lax.dynamic_slice_in_dim(proj_weight, (index % mp_size) * width, width, 1)

    row_count = query_rows.shape[0]
    head_count = width // HEAD_DIM
    root_dim = math.sqrt(HEAD_DIM)

    other_grad = swap(out_grad)

    query_heads = query_rows.reshape(row_count, head_count, HEAD_DIM)
    key_heads = key_rows.reshape(row_count, head_count, HEAD_DIM)
    value_heads = value_rows.reshape(row_count, head_count, HEAD_DIM)
    same_image = starts[:, None] == starts[None, :]
    valid_rows = (starts >= 0)[:, None]
    scores = (
        jnp.einsum("qhd,khd->hqk", query_heads, key_heads, preferred_element_type=jnp.float32)
        / root_dim
    )
    scores = jnp.where(same_image[None], scores, -jnp.inf)
    maxima = jnp.max(scores, axis=2, keepdims=True)
    weights = jnp.exp(scores - maxima)
    probabilities = weights / jnp.sum(weights, axis=2, keepdims=True)
    rounded = probabilities.astype(jnp.bfloat16)
    attended = jnp.einsum(
        "hqk,khd->qhd", rounded, value_heads, preferred_element_type=jnp.float32
    ).reshape(row_count, -1)
    attended = attended.astype(jnp.bfloat16)
    other_attended = swap(attended)

    pair_grad = pack(out_grad, other_grad)
    pair_attended = pack(attended, other_attended)
    partial = place_half(
        dot(half_of(pair_grad), weight_block(z), (((1,), (1,)), ((), ())))
    )
    terms = dot(pair_attended, proj_weight).astype(jnp.bfloat16)

    def term(index):
        return lax.dynamic_slice_in_dim(terms, (index % mp_size) * width, width, 1)

    block = pair_grad
    total = half_of(term(z + half_ring * delta))
    for step in range(1, half_ring + 1):
        block = ring(half_of(block) if step == half_ring else block)
        received = ring(total)
        product = dot(block, weight_block(z + step * (mp_size - delta)), (((1,), (1,)), ((), ())))
        if step == half_ring:
            product = place_half(product)
        partial = partial + product
        if step == 1:
            received = place_half(received)
        own = term(z + (half_ring - step) * delta)
        if step == half_ring:
            own = place_half(half_of(own))
        total = received.astype(jnp.float32) + own.astype(jnp.float32)
        if step < half_ring:
            total = total.astype(jnp.bfloat16)

    grad_pair = (partial + swap(partial.astype(jnp.bfloat16)).astype(jnp.float32)).astype(jnp.bfloat16)
    grad_attended = unpack(grad_pair)
    projected = unpack(
        (total + swap(total.astype(jnp.bfloat16)).astype(jnp.float32)).astype(jnp.bfloat16)
    )
    projected = jnp.where(valid_rows, projected, 0)

    grad_heads = grad_attended.reshape(row_count, head_count, HEAD_DIM)
    grad_value = jnp.einsum("hqk,qhd->khd", rounded, grad_heads, preferred_element_type=jnp.float32)
    grad_weights = jnp.einsum(
        "qhd,khd->hqk", grad_heads, value_heads, preferred_element_type=jnp.float32
    )
    correction = jnp.sum(probabilities * grad_weights, axis=2, keepdims=True)
    grad_scores = (probabilities * (grad_weights - correction) / root_dim).astype(jnp.bfloat16)
    grad_query = jnp.einsum(
        "hqk,khd->qhd", grad_scores, key_heads, preferred_element_type=jnp.float32
    )
    grad_key = jnp.einsum(
        "hqk,qhd->khd", grad_scores, query_heads, preferred_element_type=jnp.float32
    )

    def finish(gradient):
        return jnp.where(valid_rows, gradient.reshape(row_count, -1), 0.0).astype(jnp.bfloat16)

    return (projected, finish(grad_query), finish(grad_key), finish(grad_value))


def solution(mesh):
    placed = (P("dp", "mp"), P("dp", "mp"), P("dp", "mp"), P("mp", None), P("dp", "mp"), P())
    return jax.shard_map(
        shards,
        mesh=mesh,
        in_specs=placed,
        out_specs=(P("dp", "mp"), P("dp", "mp"), P("dp", "mp"), P("dp", "mp")),
        check_vma=False,
    )
```

```python
import math

import jax
import jax.numpy as jnp
from jax import lax
from jax.sharding import PartitionSpec as P

HEAD_DIM = 128
SLOT = 128


def ring_pairs(dp_size, mp_size, distance):
    pairs = []
    for dp in range(dp_size):
        step = distance if goes_right(dp, dp_size) else mp_size - distance
        for z in range(mp_size):
            pairs.append((dp * mp_size + z, dp * mp_size + (z + step) % mp_size))
    return pairs


def goes_right(dp, dp_size):
    return (dp // (dp_size // 2) + dp) % 2 == 0


def dot(a, b, dims=(((1,), (0,)), ((), ()))):
    return lax.dot_general(a, b, dims, preferred_element_type=jnp.float32)


def shards(query_rows, key_rows, value_rows, proj_weight, out_grad, image_starts):
    dp_size, mp_size = lax.axis_size("dp"), lax.axis_size("mp")
    near = mp_size // 4
    far = near + 1
    dp, z = lax.axis_index("dp"), lax.axis_index("mp")
    hop_perm = ring_pairs(dp_size, mp_size, 1)
    jump_perm = ring_pairs(dp_size, mp_size, far)
    swap_perm = [(i, (i + dp_size // 2) % dp_size) for i in range(dp_size)]
    right = goes_right(dp, dp_size)
    delta = jnp.where(right, 1, mp_size - 1)
    starts = lax.dynamic_index_in_dim(image_starts, dp, 0, keepdims=False)
    other_starts = lax.dynamic_index_in_dim(
        image_starts, (dp + dp_size // 2) % dp_size, 0, keepdims=False
    )
    heavy = starts[SLOT - 1] >= 0
    light_count = jnp.sum((jnp.where(heavy, other_starts, starts) >= 0).astype(jnp.int32))
    from_light = (jnp.arange(SLOT) < light_count)[:, None]
    flip = (jnp.arange(SLOT)[:, None] + jnp.arange(SLOT)[None, :] == SLOT - 1).astype(jnp.bfloat16)

    def hop(rows):
        return lax.ppermute(rows, ("dp", "mp"), hop_perm)

    def jump(rows):
        return lax.ppermute(rows, ("dp", "mp"), jump_perm)

    def swap(rows):
        return lax.ppermute(rows, "dp", swap_perm)

    def pack(own, other):
        heavy_rows = jnp.where(heavy, own, other)
        light_rows = jnp.where(heavy, other[:SLOT], own[:SLOT])
        flipped = dot(flip, heavy_rows[SLOT:]).astype(jnp.bfloat16)
        return jnp.concatenate([heavy_rows[:SLOT], jnp.where(from_light, light_rows, flipped)], 0)

    def unpack(rows):
        first = jnp.where(heavy, rows[:SLOT], rows[SLOT:])
        return jnp.concatenate([first, dot(flip, rows[SLOT:]).astype(jnp.bfloat16)], 0)

    def half_of(rows):
        return jnp.where(right, rows[:SLOT], rows[SLOT:])

    def place_half(rows):
        zeros = jnp.zeros_like(rows)
        return jnp.concatenate([jnp.where(right, rows, zeros), jnp.where(right, zeros, rows)], 0)

    width = query_rows.shape[1]

    def weight_block(index):
        return lax.dynamic_slice_in_dim(proj_weight, (index % mp_size) * width, width, 1)

    row_count = query_rows.shape[0]
    head_count = width // HEAD_DIM
    root_dim = math.sqrt(HEAD_DIM)

    other_grad = swap(out_grad)

    query_heads = query_rows.reshape(row_count, head_count, HEAD_DIM)
    key_heads = key_rows.reshape(row_count, head_count, HEAD_DIM)
    value_heads = value_rows.reshape(row_count, head_count, HEAD_DIM)
    same_image = starts[:, None] == starts[None, :]
    valid_rows = (starts >= 0)[:, None]
    scores = (
        jnp.einsum("qhd,khd->hqk", query_heads, key_heads, preferred_element_type=jnp.float32)
        / root_dim
    )
    scores = jnp.where(same_image[None], scores, -jnp.inf)
    maxima = jnp.max(scores, axis=2, keepdims=True)
    weights = jnp.exp(scores - maxima)
    probabilities = weights / jnp.sum(weights, axis=2, keepdims=True)
    rounded = probabilities.astype(jnp.bfloat16)
    attended = jnp.einsum(
        "hqk,khd->qhd", rounded, value_heads, preferred_element_type=jnp.float32
    ).reshape(row_count, -1)
    attended = attended.astype(jnp.bfloat16)
    other_attended = swap(attended)

    pair_grad = pack(out_grad, other_grad)
    pair_attended = pack(attended, other_attended)
    partial = place_half(
        dot(half_of(pair_grad), weight_block(z), (((1,), (1,)), ((), ())))
    )
    terms = dot(pair_attended, proj_weight).astype(jnp.bfloat16)

    def term(distance):
        index = z + distance * delta
        return lax.dynamic_slice_in_dim(terms, (index % mp_size) * width, width, 1)

    def product(block, distance):
        return dot(
            block, weight_block(z + distance * (mp_size - delta)), (((1,), (1,)), ((), ()))
        )

    def plus(received, distance):
        total = received.astype(jnp.float32) + term(distance).astype(jnp.float32)
        return total.astype(jnp.bfloat16)

    rows = 2 * SLOT
    near_block, far_block = hop(pair_grad), jump(pair_grad)
    sums = hop(jnp.concatenate([term(near), half_of(term(near + far - 1))], 0))
    sums = [sums[:rows], place_half(sums[rows:])]
    for step in range(1, near):
        last = step == near - 1
        partial = partial + product(near_block, step) + product(far_block, far + step - 1)
        moved = hop(jnp.concatenate([near_block, half_of(far_block) if last else far_block], 0))
        near_block, far_block = moved[:rows], moved[rows:]
        sums = [plus(sums[0], near - step), plus(sums[1], near + far - 1 - step)]
        if last:
            sums = [hop(sums[0]), jump(sums[1])]
        else:
            sums = hop(jnp.concatenate(sums, 0))
            sums = [sums[:rows], sums[rows:]]
    partial = partial + product(near_block, near) + place_half(product(far_block, near + far - 1))
    total = (
        sums[0].astype(jnp.float32)
        + sums[1].astype(jnp.float32)
        + place_half(half_of(term(0)).astype(jnp.float32))
    )

    grad_pair = (partial + swap(partial.astype(jnp.bfloat16)).astype(jnp.float32)).astype(jnp.bfloat16)
    grad_attended = unpack(grad_pair)
    projected = unpack(
        (total + swap(total.astype(jnp.bfloat16)).astype(jnp.float32)).astype(jnp.bfloat16)
    )
    projected = jnp.where(valid_rows, projected, 0)

    grad_heads = grad_attended.reshape(row_count, head_count, HEAD_DIM)
    grad_value = jnp.einsum("hqk,qhd->khd", rounded, grad_heads, preferred_element_type=jnp.float32)
    grad_weights = jnp.einsum(
        "qhd,khd->hqk", grad_heads, value_heads, preferred_element_type=jnp.float32
    )
    correction = jnp.sum(probabilities * grad_weights, axis=2, keepdims=True)
    grad_scores = (probabilities * (grad_weights - correction) / root_dim).astype(jnp.bfloat16)
    grad_query = jnp.einsum(
        "hqk,khd->qhd", grad_scores, key_heads, preferred_element_type=jnp.float32
    )
    grad_key = jnp.einsum(
        "hqk,qhd->khd", grad_scores, query_heads, preferred_element_type=jnp.float32
    )

    def finish(gradient):
        return jnp.where(valid_rows, gradient.reshape(row_count, -1), 0.0).astype(jnp.bfloat16)

    return (projected, finish(grad_query), finish(grad_key), finish(grad_value))


def solution(mesh):
    placed = (P("dp", "mp"), P("dp", "mp"), P("dp", "mp"), P("mp", None), P("dp", "mp"), P())
    return jax.shard_map(
        shards,
        mesh=mesh,
        in_specs=placed,
        out_specs=(P("dp", "mp"), P("dp", "mp"), P("dp", "mp"), P("dp", "mp")),
        check_vma=False,
    )
```

```python
import functools
import math

import jax
import jax.numpy as jnp
from jax import lax
from jax.experimental import pallas as pl
from jax.experimental.pallas import tpu as pltpu
from jax.sharding import PartitionSpec as P

HEAD_DIM = 128
SLOT = 128
ROWS = 256
VMEM_LIMIT = 20 * 1024 * 1024
FRONT_LIMIT = 58 * 1024 * 1024
IN_VMEM = pl.BlockSpec(memory_space=pltpu.VMEM)


def ring_pairs(dp_size, mp_size, distance):
    pairs = []
    for dp in range(dp_size):
        step = distance if goes_right(dp, dp_size) else mp_size - distance
        for z in range(mp_size):
            pairs.append((dp * mp_size + z, dp * mp_size + (z + step) % mp_size))
    return pairs


def goes_right(dp, dp_size):
    half = dp_size // 2
    if isinstance(dp, int):
        return (dp // half + dp) % 2 == 0
    return lax.rem(lax.div(dp, half) + dp, 2) == 0


def dot(a, b, dims=(1, 0)):
    return lax.dot_general(
        a, b, (((dims[0],), (dims[1],)), ((), ())), preferred_element_type=jnp.float32
    )


def call(kernel, outs, operands, specs=None, scratch=(), flops=0, name=None, limit=VMEM_LIMIT):
    moved = sum(math.prod(a.shape) * a.dtype.itemsize for a in (*operands, *outs))
    return pl.pallas_call(
        kernel,
        out_shape=outs,
        in_specs=specs or [IN_VMEM] * len(operands),
        out_specs=[IN_VMEM] * len(outs),
        scratch_shapes=list(scratch),
        compiler_params=pltpu.CompilerParams(vmem_limit_bytes=limit),
        cost_estimate=pl.CostEstimate(flops=flops, bytes_accessed=moved, transcendentals=0),
        name=name,
    )(*operands)


def starts_of(starts_ref):
    return starts_ref[0:1, :], starts_ref[1:2, :]


def as_column(row):
    size = row.shape[1]
    on_diagonal = lax.broadcasted_iota(jnp.int32, (size, size), 0) == lax.broadcasted_iota(
        jnp.int32, (size, size), 1
    )
    return jnp.sum(jnp.where(on_diagonal, row, 0), axis=1, keepdims=True)


def is_heavy(own):
    lanes = lax.broadcasted_iota(jnp.int32, own.shape, 1)
    return jnp.sum(jnp.where(lanes == SLOT - 1, own, 0)) >= 0


def flip_matrix():
    total = lax.broadcasted_iota(jnp.int32, (SLOT, SLOT), 0) + lax.broadcasted_iota(
        jnp.int32, (SLOT, SLOT), 1
    )
    return jnp.where(total == SLOT - 1, 1.0, 0.0).astype(jnp.bfloat16)


def packed_slots(own_starts, other_starts, own_ref, other_ref):
    heavy = is_heavy(own_starts)
    light_starts = jnp.where(heavy, other_starts, own_starts)
    light_count = jnp.sum((light_starts >= 0).astype(jnp.int32))
    from_light = lax.broadcasted_iota(jnp.int32, (SLOT, 1), 0) < light_count
    own_first, other_first = own_ref[:SLOT, :], other_ref[:SLOT, :]
    first = jnp.where(heavy, own_first, other_first)
    light = jnp.where(heavy, other_first, own_first)
    second = jnp.where(heavy, own_ref[SLOT:, :], other_ref[SLOT:, :])
    flipped = dot(flip_matrix(), second)
    second_slot = jnp.where(from_light, light.astype(jnp.float32), flipped).astype(jnp.bfloat16)
    return first, second_slot


def started(moves, sems):
    copies = [pltpu.make_async_copy(*move, sems.at[at]) for at, move in enumerate(moves)]
    for copy in copies:
        copy.start()
    return copies


def pack_kernel(own_hbm, other_hbm, starts_hbm, out_ref, own_ref, other_ref, starts_ref, sems):
    moves = [(starts_hbm, starts_ref), (own_hbm, own_ref), (other_hbm, other_ref)]
    for copy in started(moves, sems):
        copy.wait()
    first, second = packed_slots(*starts_of(starts_ref), own_ref, other_ref)
    out_ref[:SLOT, :] = first
    out_ref[SLOT:, :] = second


def pack_terms_kernel(
    dp_size,
    own_hbm,
    other_hbm,
    starts_hbm,
    held_hbm,
    out_ref,
    terms_ref,
    own_ref,
    other_ref,
    starts_ref,
    held_ref,
    sems,
):
    moves = [
        (starts_hbm, starts_ref),
        (own_hbm, own_ref),
        (other_hbm, other_ref),
        (held_hbm, held_ref),
    ]
    copies = started(moves, sems)
    right = goes_right(lax.axis_index("dp"), dp_size)
    for copy in copies[:3]:
        copy.wait()
    first, second = packed_slots(*starts_of(starts_ref), own_ref, other_ref)
    out_ref[:SLOT, :] = first
    out_ref[SLOT:, :] = second
    half = jnp.where(right, first, second)
    copies[3].wait()
    terms_ref[:SLOT, :] = dot(first, held_ref[0]).astype(jnp.bfloat16)
    terms_ref[SLOT:ROWS, :] = dot(second, held_ref[0]).astype(jnp.bfloat16)
    terms_ref[ROWS:, :] = dot(half, held_ref[1]).astype(jnp.bfloat16)


def probabilities_of(query, key, same_image):
    scores = dot(query, key, (1, 1)) / math.sqrt(HEAD_DIM)
    scores = jnp.where(same_image, scores, -jnp.inf)
    weights = jnp.exp(scores - jnp.max(scores, axis=1, keepdims=True))
    return weights * (1.0 / jnp.sum(weights, axis=1, keepdims=True))


def forward_kernel(
    dp_size,
    mp_size,
    distances,
    query_hbm,
    key_hbm,
    value_hbm,
    weight_hbm,
    starts_ref,
    out_ref,
    held_ref,
    pair_starts_ref,
    query_ref,
    key_ref,
    value_ref,
    sems,
):
    width = query_ref.shape[1]
    dp, z = lax.axis_index("dp"), lax.axis_index("mp")
    right = goes_right(dp, dp_size)
    moves = [
        (query_hbm, query_ref),
        (key_hbm, key_ref),
        (value_hbm, value_ref),
    ]
    for slot, distance in enumerate(distances):
        index = lax.rem(z + jnp.where(right, distance, mp_size - distance), mp_size)
        columns = pl.ds(pl.multiple_of(index * width, 128), width)
        moves.append((weight_hbm.at[:, columns], held_ref.at[slot]))
    copies = started(moves, sems)
    own = starts_ref[pl.ds(dp, 1), :]
    pair_starts_ref[0:1, :] = own
    pair_starts_ref[1:2, :] = starts_ref[pl.ds(lax.rem(dp + dp_size // 2, dp_size), 1), :]
    same_image = as_column(own) == own
    for copy in copies[:3]:
        copy.wait()
    for head in range(width // HEAD_DIM):
        at = slice(head * HEAD_DIM, (head + 1) * HEAD_DIM)
        rounded = probabilities_of(query_ref[:, at], key_ref[:, at], same_image).astype(jnp.bfloat16)
        out_ref[:, at] = dot(rounded, value_ref[:, at]).astype(jnp.bfloat16)
    for copy in copies[3:]:
        copy.wait()


def unpacked(heavy, first, second):
    own_first = jnp.where(heavy, first, second)
    return own_first, dot(flip_matrix(), second.astype(jnp.bfloat16))


def backward_kernel(
    query_ref,
    key_ref,
    value_ref,
    partial_ref,
    other_ref,
    starts_ref,
    grad_query_ref,
    grad_key_ref,
    grad_value_ref,
    grad_ref,
):
    own, _ = starts_of(starts_ref)
    column = as_column(own)
    same_image = column == own
    valid = column >= 0
    pair = partial_ref[...] + other_ref[...].astype(jnp.float32)
    low, high = unpacked(is_heavy(own), pair[:SLOT], pair[SLOT:])
    grad_ref[:SLOT, :] = low.astype(jnp.bfloat16)
    grad_ref[SLOT:, :] = high.astype(jnp.bfloat16)
    for head in range(query_ref.shape[1] // HEAD_DIM):
        at = slice(head * HEAD_DIM, (head + 1) * HEAD_DIM)
        query, key, value, grad = query_ref[:, at], key_ref[:, at], value_ref[:, at], grad_ref[:, at]
        probabilities = probabilities_of(query, key, same_image)
        rounded = probabilities.astype(jnp.bfloat16)
        grad_value = dot(rounded, grad, (0, 0))
        grad_weights = dot(grad, value, (1, 1))
        correction = jnp.sum(probabilities * grad_weights, axis=1, keepdims=True)
        grad_scores = (probabilities * (grad_weights - correction) / math.sqrt(HEAD_DIM)).astype(
            jnp.bfloat16
        )
        grad_query = dot(grad_scores, key)
        grad_key = dot(grad_scores, query, (0, 0))
        grad_query_ref[:, at] = jnp.where(valid, grad_query, 0.0).astype(jnp.bfloat16)
        grad_key_ref[:, at] = jnp.where(valid, grad_key, 0.0).astype(jnp.bfloat16)
        grad_value_ref[:, at] = jnp.where(valid, grad_value, 0.0).astype(jnp.bfloat16)


def finish_kernel(total_ref, other_ref, starts_ref, out_ref):
    own, _ = starts_of(starts_ref)
    valid = as_column(own) >= 0
    pair = total_ref[...] + other_ref[...].astype(jnp.float32)
    low, high = unpacked(is_heavy(own), pair[:SLOT], pair[SLOT:])
    out_ref[:SLOT, :] = jnp.where(valid[:SLOT], low, 0.0).astype(jnp.bfloat16)
    out_ref[SLOT:, :] = jnp.where(valid[SLOT:], high, 0.0).astype(jnp.bfloat16)


def shards(query_rows, key_rows, value_rows, proj_weight, out_grad, image_starts):
    dp_size, mp_size = lax.axis_size("dp"), lax.axis_size("mp")
    width = query_rows.shape[1]
    near = mp_size // 4
    far = near + 1
    dp, z = lax.axis_index("dp"), lax.axis_index("mp")
    hop_perm = ring_pairs(dp_size, mp_size, 1)
    jump_perm = ring_pairs(dp_size, mp_size, far)
    swap_perm = [(i, (i + dp_size // 2) % dp_size) for i in range(dp_size)]
    right = goes_right(dp, dp_size)
    delta = jnp.where(right, 1, mp_size - 1)
    rows_type = jax.ShapeDtypeStruct((ROWS, width), jnp.bfloat16)
    half_type = jax.ShapeDtypeStruct((ROWS + SLOT, width), jnp.bfloat16)

    def hop(rows):
        return lax.ppermute(rows, ("dp", "mp"), hop_perm)

    def jump(rows):
        return lax.ppermute(rows, ("dp", "mp"), jump_perm)

    def swap(rows):
        return lax.ppermute(rows, "dp", swap_perm)

    def half_of(rows):
        return jnp.where(right, rows[:SLOT], rows[SLOT:])

    def place_half(rows):
        zeros = jnp.zeros_like(rows)
        return jnp.concatenate([jnp.where(right, rows, zeros), jnp.where(right, zeros, rows)], 0)

    def block_of(array, index):
        return lax.dynamic_slice_in_dim(array, lax.rem(index, mp_size) * width, width, 1)

    other_out_grad = swap(out_grad)
    in_hbm = pl.BlockSpec(memory_space=pltpu.HBM)
    in_any = pl.BlockSpec(memory_space=pl.ANY)
    held_type = jax.ShapeDtypeStruct((2, width, width), jnp.bfloat16)
    starts_type = jax.ShapeDtypeStruct((2, ROWS), jnp.int32)
    row_buffer = pltpu.VMEM((ROWS, width), jnp.bfloat16)
    starts_buffer = pltpu.VMEM((2, ROWS), jnp.int32)
    attended, held, starts = call(
        functools.partial(forward_kernel, dp_size, mp_size, (near, near + far - 1)),
        [rows_type, held_type, starts_type],
        (query_rows, key_rows, value_rows, proj_weight, image_starts),
        specs=[in_hbm] * 4 + [IN_VMEM],
        scratch=[row_buffer] * 3 + [pltpu.SemaphoreType.DMA((5,))],
        flops=4 * ROWS * ROWS * width,
        name="attention_forward",
        limit=FRONT_LIMIT,
    )
    other_attended = swap(attended)
    (pair_grad,) = call(
        pack_kernel,
        [rows_type],
        (out_grad, other_out_grad, starts),
        specs=[in_hbm, in_any, in_hbm],
        scratch=[row_buffer] * 2 + [starts_buffer, pltpu.SemaphoreType.DMA((3,))],
        name="pack_out_grad",
        limit=FRONT_LIMIT,
    )
    near_block, far_block = hop(pair_grad), jump(pair_grad)
    pair_attended, first_terms = call(
        functools.partial(pack_terms_kernel, dp_size),
        [rows_type, half_type],
        (attended, other_attended, starts, held),
        specs=[in_hbm, in_any, in_hbm, in_hbm],
        scratch=[row_buffer] * 2
        + [
            starts_buffer,
            pltpu.VMEM((2, width, width), jnp.bfloat16),
            pltpu.SemaphoreType.DMA((4,)),
        ],
        name="pack_attended",
        limit=FRONT_LIMIT,
    )
    sums = hop(first_terms)
    sums = [sums[:ROWS], place_half(sums[ROWS:])]

    def term(distance):
        return dot(pair_attended, block_of(proj_weight, z + distance * delta))

    def product(block, distance):
        return dot(block, block_of(proj_weight, z + distance * (mp_size - delta)), (1, 1))

    def plus(received, distance):
        return (received.astype(jnp.float32) + term(distance)).astype(jnp.bfloat16)

    partial = place_half(product(half_of(pair_grad), 0))
    for step in range(1, near):
        last = step == near - 1
        partial = partial + product(near_block, step) + product(far_block, far + step - 1)
        moved = hop(jnp.concatenate([near_block, half_of(far_block) if last else far_block], 0))
        near_block, far_block = moved[:ROWS], moved[ROWS:]
        sums = [plus(sums[0], near - step), plus(sums[1], near + far - 1 - step)]
        if last:
            sums = [hop(sums[0]), jump(sums[1])]
        else:
            sums = hop(jnp.concatenate(sums, 0))
            sums = [sums[:ROWS], sums[ROWS:]]
    partial = partial + product(near_block, near) + place_half(product(far_block, near + far - 1))
    near_sum, partial = lax.optimization_barrier((sums[0], partial))
    other_partial = swap(partial.astype(jnp.bfloat16))
    last_sum, other_partial = lax.optimization_barrier((sums[1], other_partial))
    total = (
        near_sum.astype(jnp.float32)
        + last_sum.astype(jnp.float32)
        + place_half(dot(half_of(pair_attended), block_of(proj_weight, z)))
    )
    other_total = swap(total.astype(jnp.bfloat16))
    grads = call(
        backward_kernel,
        [rows_type] * 3,
        (query_rows, key_rows, value_rows, partial, other_partial, starts),
        scratch=[pltpu.VMEM((ROWS, width), jnp.bfloat16)],
        flops=12 * ROWS * ROWS * width,
        name="attention_backward",
    )
    (projected,) = call(
        finish_kernel,
        [rows_type],
        (total, other_total, starts),
        name="finish_projected",
    )
    return (projected, *grads)


def solution(mesh):
    placed = (P("dp", "mp"), P("dp", "mp"), P("dp", "mp"), P("mp", None), P("dp", "mp"), P())
    return jax.shard_map(
        shards,
        mesh=mesh,
        in_specs=placed,
        out_specs=(P("dp", "mp"), P("dp", "mp"), P("dp", "mp"), P("dp", "mp")),
        check_vma=False,
    )
```

```python
import functools
import math

import jax
import jax.numpy as jnp
from jax import lax
from jax.experimental import pallas as pl
from jax.experimental.pallas import tpu as pltpu
from jax.sharding import PartitionSpec as P

HEAD_DIM = 128
SLOT = 128
ROWS = 256
VMEM_LIMIT = 20 * 1024 * 1024
FRONT_LIMIT = 58 * 1024 * 1024
IN_VMEM = pl.BlockSpec(memory_space=pltpu.VMEM)


def ring_pairs(dp_size, mp_size, distance):
    pairs = []
    for dp in range(dp_size):
        step = distance if goes_right(dp, dp_size) else mp_size - distance
        for z in range(mp_size):
            pairs.append((dp * mp_size + z, dp * mp_size + (z + step) % mp_size))
    return pairs


def goes_right(dp, dp_size):
    half = dp_size // 2
    if isinstance(dp, int):
        return (dp // half + dp) % 2 == 0
    return lax.rem(lax.div(dp, half) + dp, 2) == 0


def dot(a, b, dims=(1, 0)):
    return lax.dot_general(
        a, b, (((dims[0],), (dims[1],)), ((), ())), preferred_element_type=jnp.float32
    )


def call(kernel, outs, operands, specs=None, scratch=(), flops=0, name=None, limit=VMEM_LIMIT):
    moved = sum(math.prod(a.shape) * a.dtype.itemsize for a in (*operands, *outs))
    return pl.pallas_call(
        kernel,
        out_shape=outs,
        in_specs=specs or [IN_VMEM] * len(operands),
        out_specs=[IN_VMEM] * len(outs),
        scratch_shapes=list(scratch),
        compiler_params=pltpu.CompilerParams(vmem_limit_bytes=limit),
        cost_estimate=pl.CostEstimate(flops=flops, bytes_accessed=moved, transcendentals=0),
        name=name,
    )(*operands)


def starts_of(starts_ref):
    return starts_ref[0:1, :], starts_ref[1:2, :]


def as_column(row):
    size = row.shape[1]
    on_diagonal = lax.broadcasted_iota(jnp.int32, (size, size), 0) == lax.broadcasted_iota(
        jnp.int32, (size, size), 1
    )
    return jnp.sum(jnp.where(on_diagonal, row, 0), axis=1, keepdims=True)


def is_heavy(own):
    lanes = lax.broadcasted_iota(jnp.int32, own.shape, 1)
    return jnp.sum(jnp.where(lanes == SLOT - 1, own, 0)) >= 0


def flip_matrix():
    total = lax.broadcasted_iota(jnp.int32, (SLOT, SLOT), 0) + lax.broadcasted_iota(
        jnp.int32, (SLOT, SLOT), 1
    )
    return jnp.where(total == SLOT - 1, 1.0, 0.0).astype(jnp.bfloat16)


def packed_slots(own_starts, other_starts, own_ref, other_ref):
    heavy = is_heavy(own_starts)
    light_starts = jnp.where(heavy, other_starts, own_starts)
    light_count = jnp.sum((light_starts >= 0).astype(jnp.int32))
    from_light = lax.broadcasted_iota(jnp.int32, (SLOT, 1), 0) < light_count
    own_first, other_first = own_ref[:SLOT, :], other_ref[:SLOT, :]
    first = jnp.where(heavy, own_first, other_first)
    light = jnp.where(heavy, other_first, own_first)
    second = jnp.where(heavy, own_ref[SLOT:, :], other_ref[SLOT:, :])
    flipped = dot(flip_matrix(), second)
    second_slot = jnp.where(from_light, light.astype(jnp.float32), flipped).astype(jnp.bfloat16)
    return first, second_slot


def pack_kernel(own_ref, other_ref, starts_ref, out_ref):
    first, second = packed_slots(*starts_of(starts_ref), own_ref, other_ref)
    out_ref[:SLOT, :] = first
    out_ref[SLOT:, :] = second


def pack_terms_kernel(
    dp_size,
    mp_size,
    distances,
    own_ref,
    other_ref,
    starts_ref,
    weight_ref,
    earlier_ref,
    out_ref,
    terms_ref,
):
    del earlier_ref
    right = goes_right(lax.axis_index("dp"), dp_size)
    first, second = packed_slots(*starts_of(starts_ref), own_ref, other_ref)
    out_ref[:SLOT, :] = first
    out_ref[SLOT:, :] = second
    half = jnp.where(right, first, second)

    near_weight, far_weight = weights_at(dp_size, mp_size, distances, weight_ref)
    terms_ref[:SLOT, :] = dot(first, near_weight).astype(jnp.bfloat16)
    terms_ref[SLOT:ROWS, :] = dot(second, near_weight).astype(jnp.bfloat16)
    terms_ref[ROWS:, :] = dot(half, far_weight).astype(jnp.bfloat16)


def weights_at(dp_size, mp_size, distances, weight_ref):
    width = weight_ref.shape[0]
    right = goes_right(lax.axis_index("dp"), dp_size)
    found = []
    for distance in distances:
        ahead = jnp.where(right, distance, mp_size - distance)
        index = lax.rem(lax.axis_index("mp") + ahead, mp_size)
        found.append(weight_ref[:, pl.ds(pl.multiple_of(index * width, 128), width)])
    return found


def add_terms_kernel(dp_size, mp_size, distances, sums_ref, rows_ref, weight_ref, *out_refs):
    near_weight, far_weight = weights_at(dp_size, mp_size, distances, weight_ref)
    near_term, far_term = dot(rows_ref[...], near_weight), dot(rows_ref[...], far_weight)
    near_sum = sums_ref[:ROWS, :].astype(jnp.float32) + near_term
    if sums_ref.shape[0] == 2 * ROWS:
        far_sum = sums_ref[ROWS:, :].astype(jnp.float32) + far_term
    else:
        right = goes_right(lax.axis_index("dp"), dp_size)
        half = sums_ref[ROWS:, :].astype(jnp.float32)
        first = jnp.where(right, half, 0.0) + far_term[:SLOT]
        second = jnp.where(right, 0.0, half) + far_term[SLOT:]
        far_sum = jnp.concatenate([first, second], 0)
    if len(out_refs) == 2:
        out_refs[0][...] = near_sum.astype(jnp.bfloat16)
        out_refs[1][...] = far_sum.astype(jnp.bfloat16)
    else:
        out_refs[0][:ROWS, :] = near_sum.astype(jnp.bfloat16)
        out_refs[0][ROWS:, :] = far_sum.astype(jnp.bfloat16)


def join_kernel(near_ref, far_ref, earlier_ref, out_ref):
    del earlier_ref
    out_ref[:ROWS, :] = near_ref[...]
    out_ref[ROWS:, :] = far_ref[...]


def probabilities_of(query, key, same_image):
    scores = dot(query, key, (1, 1)) / math.sqrt(HEAD_DIM)
    scores = jnp.where(same_image, scores, -jnp.inf)
    weights = jnp.exp(scores - jnp.max(scores, axis=1, keepdims=True))
    return weights * (1.0 / jnp.sum(weights, axis=1, keepdims=True))


def forward_kernel(dp_size, query_ref, key_ref, value_ref, starts_ref, out_ref, pair_starts_ref):
    width = query_ref.shape[1]
    dp = lax.axis_index("dp")
    own = starts_ref[pl.ds(dp, 1), :]
    pair_starts_ref[0:1, :] = own
    pair_starts_ref[1:2, :] = starts_ref[pl.ds(lax.rem(dp + dp_size // 2, dp_size), 1), :]
    same_image = as_column(own) == own
    for head in range(width // HEAD_DIM):
        at = slice(head * HEAD_DIM, (head + 1) * HEAD_DIM)
        rounded = probabilities_of(query_ref[:, at], key_ref[:, at], same_image).astype(jnp.bfloat16)
        out_ref[:, at] = dot(rounded, value_ref[:, at]).astype(jnp.bfloat16)


def unpacked(heavy, first, second):
    own_first = jnp.where(heavy, first, second)
    return own_first, dot(flip_matrix(), second.astype(jnp.bfloat16))


def backward_kernel(
    query_ref,
    key_ref,
    value_ref,
    partial_ref,
    other_ref,
    starts_ref,
    grad_query_ref,
    grad_key_ref,
    grad_value_ref,
    grad_ref,
):
    own, _ = starts_of(starts_ref)
    column = as_column(own)
    same_image = column == own
    valid = column >= 0
    pair = partial_ref[...] + other_ref[...].astype(jnp.float32)
    low, high = unpacked(is_heavy(own), pair[:SLOT], pair[SLOT:])
    grad_ref[:SLOT, :] = low.astype(jnp.bfloat16)
    grad_ref[SLOT:, :] = high.astype(jnp.bfloat16)
    for head in range(query_ref.shape[1] // HEAD_DIM):
        at = slice(head * HEAD_DIM, (head + 1) * HEAD_DIM)
        query, key, value, grad = query_ref[:, at], key_ref[:, at], value_ref[:, at], grad_ref[:, at]
        probabilities = probabilities_of(query, key, same_image)
        rounded = probabilities.astype(jnp.bfloat16)
        grad_value = dot(rounded, grad, (0, 0))
        grad_weights = dot(grad, value, (1, 1))
        correction = jnp.sum(probabilities * grad_weights, axis=1, keepdims=True)
        grad_scores = (probabilities * (grad_weights - correction) / math.sqrt(HEAD_DIM)).astype(
            jnp.bfloat16
        )
        grad_query = dot(grad_scores, key)
        grad_key = dot(grad_scores, query, (0, 0))
        grad_query_ref[:, at] = jnp.where(valid, grad_query, 0.0).astype(jnp.bfloat16)
        grad_key_ref[:, at] = jnp.where(valid, grad_key, 0.0).astype(jnp.bfloat16)
        grad_value_ref[:, at] = jnp.where(valid, grad_value, 0.0).astype(jnp.bfloat16)


def finish_kernel(total_ref, other_ref, starts_ref, out_ref):
    own, _ = starts_of(starts_ref)
    valid = as_column(own) >= 0
    pair = total_ref[...] + other_ref[...].astype(jnp.float32)
    low, high = unpacked(is_heavy(own), pair[:SLOT], pair[SLOT:])
    out_ref[:SLOT, :] = jnp.where(valid[:SLOT], low, 0.0).astype(jnp.bfloat16)
    out_ref[SLOT:, :] = jnp.where(valid[SLOT:], high, 0.0).astype(jnp.bfloat16)


def shards(query_rows, key_rows, value_rows, proj_weight, out_grad, image_starts):
    dp_size, mp_size = lax.axis_size("dp"), lax.axis_size("mp")
    width = query_rows.shape[1]
    near = mp_size // 4
    far = near + 1
    dp, z = lax.axis_index("dp"), lax.axis_index("mp")
    hop_perm = ring_pairs(dp_size, mp_size, 1)
    jump_perm = ring_pairs(dp_size, mp_size, far)
    swap_perm = [(i, (i + dp_size // 2) % dp_size) for i in range(dp_size)]
    right = goes_right(dp, dp_size)
    delta = jnp.where(right, 1, mp_size - 1)
    rows_type = jax.ShapeDtypeStruct((ROWS, width), jnp.bfloat16)
    half_type = jax.ShapeDtypeStruct((ROWS + SLOT, width), jnp.bfloat16)

    def hop(rows):
        return lax.ppermute(rows, ("dp", "mp"), hop_perm)

    def jump(rows):
        return lax.ppermute(rows, ("dp", "mp"), jump_perm)

    def swap(rows):
        return lax.ppermute(rows, "dp", swap_perm)

    def half_of(rows):
        return jnp.where(right, rows[:SLOT], rows[SLOT:])

    def place_half(rows):
        zeros = jnp.zeros_like(rows)
        return jnp.concatenate([jnp.where(right, rows, zeros), jnp.where(right, zeros, rows)], 0)

    def block_of(array, index):
        return lax.dynamic_slice_in_dim(array, lax.rem(index, mp_size) * width, width, 1)

    other_out_grad = swap(out_grad)
    in_any = pl.BlockSpec(memory_space=pl.ANY)
    attended, starts = call(
        functools.partial(forward_kernel, dp_size),
        [rows_type, jax.ShapeDtypeStruct((2, ROWS), jnp.int32)],
        (query_rows, key_rows, value_rows, image_starts),
        flops=4 * ROWS * ROWS * width,
        name="attention_forward",
    )
    other_attended = swap(attended)
    (pair_grad,) = call(
        pack_kernel, [rows_type], (out_grad, other_out_grad, starts), name="pack_out_grad"
    )
    near_block, far_block = hop(pair_grad), jump(pair_grad)
    pair_attended, first_terms = call(
        functools.partial(pack_terms_kernel, dp_size, mp_size, (near, near + far - 1)),
        [rows_type, half_type],
        (attended, other_attended, starts, proj_weight, pair_grad),
        specs=[IN_VMEM] * 4 + [in_any],
        name="pack_attended",
    )

    def product(block, distance):
        return dot(block, block_of(proj_weight, z + distance * (mp_size - delta)), (1, 1))

    def add_terms(sums, step):
        distances = (near - step, near + far - 1 - step)
        joined = jax.ShapeDtypeStruct((2 * ROWS, width), jnp.bfloat16)
        return call(
            functools.partial(add_terms_kernel, dp_size, mp_size, distances),
            [rows_type, rows_type] if step == near - 1 else [joined],
            (sums, pair_attended, proj_weight),
            flops=4 * ROWS * width * width,
            name="add_terms",
        )

    sums = hop(first_terms)
    for step in range(1, near - 1):
        sums = hop(*add_terms(sums, step))
        if step == 1:
            (moved,) = call(
                join_kernel,
                [jax.ShapeDtypeStruct((2 * ROWS, width), jnp.bfloat16)],
                (near_block, far_block, first_terms),
                specs=[IN_VMEM] * 2 + [in_any],
                name="join_out_grad",
            )
    near_sum, last_sum = add_terms(sums, near - 1)
    last_sum, near_sum = jump(last_sum), hop(near_sum)

    partial = place_half(product(half_of(pair_grad), 0))
    for step in range(1, near):
        near_block, far_block = moved[:ROWS], moved[ROWS:]
        partial = partial + product(near_block, step) + product(far_block, far + step - 1)
        if step == near - 1:
            moved = jnp.concatenate([near_block, half_of(far_block)], 0)
        moved = hop(moved)
    near_block, far_block = moved[:ROWS], moved[ROWS:]
    partial = partial + product(near_block, near) + place_half(product(far_block, near + far - 1))
    other_partial = swap(partial.astype(jnp.bfloat16))
    last_sum, other_partial = lax.optimization_barrier((last_sum, other_partial))
    total = (
        near_sum.astype(jnp.float32)
        + last_sum.astype(jnp.float32)
        + place_half(dot(half_of(pair_attended), block_of(proj_weight, z)))
    )
    other_total = swap(total.astype(jnp.bfloat16))
    grads = call(
        backward_kernel,
        [rows_type] * 3,
        (query_rows, key_rows, value_rows, partial, other_partial, starts),
        scratch=[pltpu.VMEM((ROWS, width), jnp.bfloat16)],
        flops=12 * ROWS * ROWS * width,
        name="attention_backward",
    )
    (projected,) = call(
        finish_kernel,
        [rows_type],
        (total, other_total, starts),
        name="finish_projected",
    )
    return (projected, *grads)


def solution(mesh):
    placed = (P("dp", "mp"), P("dp", "mp"), P("dp", "mp"), P("mp", None), P("dp", "mp"), P())
    return jax.shard_map(
        shards,
        mesh=mesh,
        in_specs=placed,
        out_specs=(P("dp", "mp"), P("dp", "mp"), P("dp", "mp"), P("dp", "mp")),
        check_vma=False,
    )
```

```python
import functools
import math

import jax
import jax.numpy as jnp
from jax import lax
from jax.experimental import pallas as pl
from jax.experimental.pallas import tpu as pltpu
from jax.sharding import PartitionSpec as P

HEAD_DIM = 128
SLOT = 128
ROWS = 256
VMEM_LIMIT = 20 * 1024 * 1024
FRONT_LIMIT = 54600 * 1024
IN_VMEM = pl.BlockSpec(memory_space=pltpu.VMEM)


def ring_pairs(dp_size, mp_size, distance):
    pairs = []
    for dp in range(dp_size):
        step = distance if goes_right(dp, dp_size) else mp_size - distance
        for z in range(mp_size):
            pairs.append((dp * mp_size + z, dp * mp_size + (z + step) % mp_size))
    return pairs


def goes_right(dp, dp_size):
    half = dp_size // 2
    if isinstance(dp, int):
        return (dp // half + dp) % 2 == 0
    return lax.rem(lax.div(dp, half) + dp, 2) == 0


def dot(a, b, dims=(1, 0)):
    return lax.dot_general(
        a, b, (((dims[0],), (dims[1],)), ((), ())), preferred_element_type=jnp.float32
    )


def call(kernel, outs, operands, specs=None, scratch=(), flops=0, name=None, limit=VMEM_LIMIT):
    moved = sum(math.prod(a.shape) * a.dtype.itemsize for a in (*operands, *outs))
    return pl.pallas_call(
        kernel,
        out_shape=outs,
        in_specs=specs or [IN_VMEM] * len(operands),
        out_specs=[IN_VMEM] * len(outs),
        scratch_shapes=list(scratch),
        compiler_params=pltpu.CompilerParams(vmem_limit_bytes=limit),
        cost_estimate=pl.CostEstimate(flops=flops, bytes_accessed=moved, transcendentals=0),
        name=name,
    )(*operands)


def starts_of(starts_ref):
    return starts_ref[0:1, :], starts_ref[1:2, :]


def as_column(row):
    size = row.shape[1]
    on_diagonal = lax.broadcasted_iota(jnp.int32, (size, size), 0) == lax.broadcasted_iota(
        jnp.int32, (size, size), 1
    )
    return jnp.sum(jnp.where(on_diagonal, row, 0), axis=1, keepdims=True)


def is_heavy(own):
    lanes = lax.broadcasted_iota(jnp.int32, own.shape, 1)
    return jnp.sum(jnp.where(lanes == SLOT - 1, own, 0)) >= 0


def flip_matrix():
    total = lax.broadcasted_iota(jnp.int32, (SLOT, SLOT), 0) + lax.broadcasted_iota(
        jnp.int32, (SLOT, SLOT), 1
    )
    return jnp.where(total == SLOT - 1, 1.0, 0.0).astype(jnp.bfloat16)


def packed_slots(own_starts, other_starts, own_ref, other_ref):
    heavy = is_heavy(own_starts)
    light_starts = jnp.where(heavy, other_starts, own_starts)
    light_count = jnp.sum((light_starts >= 0).astype(jnp.int32))
    from_light = lax.broadcasted_iota(jnp.int32, (SLOT, 1), 0) < light_count
    own_first, other_first = own_ref[:SLOT, :], other_ref[:SLOT, :]
    first = jnp.where(heavy, own_first, other_first)
    light = jnp.where(heavy, other_first, own_first)
    second = jnp.where(heavy, own_ref[SLOT:, :], other_ref[SLOT:, :])
    flipped = dot(flip_matrix(), second)
    second_slot = jnp.where(from_light, light.astype(jnp.float32), flipped).astype(jnp.bfloat16)
    return first, second_slot


def pack_kernel(own_ref, other_ref, starts_ref, out_ref):
    first, second = packed_slots(*starts_of(starts_ref), own_ref, other_ref)
    out_ref[:SLOT, :] = first
    out_ref[SLOT:, :] = second


def pack_terms_kernel(
    dp_size, own_ref, other_ref, starts_ref, held_ref, earlier_ref, out_ref, terms_ref
):
    del earlier_ref
    right = goes_right(lax.axis_index("dp"), dp_size)
    first, second = packed_slots(*starts_of(starts_ref), own_ref, other_ref)
    out_ref[:SLOT, :] = first
    out_ref[SLOT:, :] = second
    half = jnp.where(right, first, second)
    terms_ref[:SLOT, :] = dot(first, held_ref[0]).astype(jnp.bfloat16)
    terms_ref[SLOT:ROWS, :] = dot(second, held_ref[0]).astype(jnp.bfloat16)
    terms_ref[ROWS:, :] = dot(half, held_ref[1]).astype(jnp.bfloat16)


def weights_at(dp_size, mp_size, distances, weight_ref):
    width = weight_ref.shape[0]
    right = goes_right(lax.axis_index("dp"), dp_size)
    found = []
    for distance in distances:
        ahead = jnp.where(right, distance, mp_size - distance)
        index = lax.rem(lax.axis_index("mp") + ahead, mp_size)
        found.append(weight_ref[:, pl.ds(pl.multiple_of(index * width, 128), width)])
    return found


def add_terms_kernel(dp_size, mp_size, distances, sums_ref, rows_ref, weight_ref, *out_refs):
    near_weight, far_weight = weights_at(dp_size, mp_size, distances, weight_ref)
    near_term, far_term = dot(rows_ref[...], near_weight), dot(rows_ref[...], far_weight)
    near_sum = sums_ref[:ROWS, :].astype(jnp.float32) + near_term
    if sums_ref.shape[0] == 2 * ROWS:
        far_sum = sums_ref[ROWS:, :].astype(jnp.float32) + far_term
    else:
        right = goes_right(lax.axis_index("dp"), dp_size)
        half = sums_ref[ROWS:, :].astype(jnp.float32)
        first = jnp.where(right, half, 0.0) + far_term[:SLOT]
        second = jnp.where(right, 0.0, half) + far_term[SLOT:]
        far_sum = jnp.concatenate([first, second], 0)
    if len(out_refs) == 2:
        out_refs[0][...] = near_sum.astype(jnp.bfloat16)
        out_refs[1][...] = far_sum.astype(jnp.bfloat16)
    else:
        out_refs[0][:ROWS, :] = near_sum.astype(jnp.bfloat16)
        out_refs[0][ROWS:, :] = far_sum.astype(jnp.bfloat16)


def join_kernel(near_ref, far_ref, earlier_ref, out_ref):
    del earlier_ref
    out_ref[:ROWS, :] = near_ref[...]
    out_ref[ROWS:, :] = far_ref[...]


def probabilities_of(query, key, same_image):
    scores = dot(query, key, (1, 1)) / math.sqrt(HEAD_DIM)
    scores = jnp.where(same_image, scores, -jnp.inf)
    weights = jnp.exp(scores - jnp.max(scores, axis=1, keepdims=True))
    return weights * (1.0 / jnp.sum(weights, axis=1, keepdims=True))


def forward_kernel(
    dp_size,
    mp_size,
    distances,
    query_hbm,
    key_hbm,
    value_hbm,
    out_grad_hbm,
    weight_hbm,
    starts_hbm,
    out_ref,
    out_grad_ref,
    held_ref,
    pair_starts_ref,
    query_ref,
    key_ref,
    value_ref,
    starts_ref,
    sems,
):
    width = query_ref.shape[1]
    dp, z = lax.axis_index("dp"), lax.axis_index("mp")
    right = goes_right(dp, dp_size)
    moves = [
        (starts_hbm, starts_ref),
        (query_hbm, query_ref),
        (key_hbm, key_ref),
        (value_hbm, value_ref),
        (out_grad_hbm, out_grad_ref),
    ]
    for slot, distance in enumerate(distances):
        index = lax.rem(z + jnp.where(right, distance, mp_size - distance), mp_size)
        columns = pl.ds(pl.multiple_of(index * width, 128), width)
        moves.append((weight_hbm.at[:, columns], held_ref.at[slot]))
    copies = [pltpu.make_async_copy(*move, sems.at[at]) for at, move in enumerate(moves)]
    for copy in copies:
        copy.start()
    copies[0].wait()
    own = starts_ref[pl.ds(dp, 1), :]
    pair_starts_ref[0:1, :] = own
    pair_starts_ref[1:2, :] = starts_ref[pl.ds(lax.rem(dp + dp_size // 2, dp_size), 1), :]
    for copy in copies[1:4]:
        copy.wait()
    same_image = as_column(own) == own
    for head in range(width // HEAD_DIM):
        at = slice(head * HEAD_DIM, (head + 1) * HEAD_DIM)
        rounded = probabilities_of(query_ref[:, at], key_ref[:, at], same_image).astype(jnp.bfloat16)
        out_ref[:, at] = dot(rounded, value_ref[:, at]).astype(jnp.bfloat16)
    for copy in copies[4:]:
        copy.wait()


def unpacked(heavy, first, second):
    own_first = jnp.where(heavy, first, second)
    return own_first, dot(flip_matrix(), second.astype(jnp.bfloat16))


def backward_kernel(
    query_ref,
    key_ref,
    value_ref,
    partial_ref,
    other_ref,
    starts_ref,
    grad_query_ref,
    grad_key_ref,
    grad_value_ref,
    grad_ref,
):
    own, _ = starts_of(starts_ref)
    column = as_column(own)
    same_image = column == own
    valid = column >= 0
    pair = partial_ref[...] + other_ref[...].astype(jnp.float32)
    low, high = unpacked(is_heavy(own), pair[:SLOT], pair[SLOT:])
    grad_ref[:SLOT, :] = low.astype(jnp.bfloat16)
    grad_ref[SLOT:, :] = high.astype(jnp.bfloat16)
    for head in range(query_ref.shape[1] // HEAD_DIM):
        at = slice(head * HEAD_DIM, (head + 1) * HEAD_DIM)
        query, key, value, grad = query_ref[:, at], key_ref[:, at], value_ref[:, at], grad_ref[:, at]
        probabilities = probabilities_of(query, key, same_image)
        rounded = probabilities.astype(jnp.bfloat16)
        grad_value = dot(rounded, grad, (0, 0))
        grad_weights = dot(grad, value, (1, 1))
        correction = jnp.sum(probabilities * grad_weights, axis=1, keepdims=True)
        grad_scores = (probabilities * (grad_weights - correction) / math.sqrt(HEAD_DIM)).astype(
            jnp.bfloat16
        )
        grad_query = dot(grad_scores, key)
        grad_key = dot(grad_scores, query, (0, 0))
        grad_query_ref[:, at] = jnp.where(valid, grad_query, 0.0).astype(jnp.bfloat16)
        grad_key_ref[:, at] = jnp.where(valid, grad_key, 0.0).astype(jnp.bfloat16)
        grad_value_ref[:, at] = jnp.where(valid, grad_value, 0.0).astype(jnp.bfloat16)


def finish_kernel(total_ref, other_ref, starts_ref, out_ref):
    own, _ = starts_of(starts_ref)
    valid = as_column(own) >= 0
    pair = total_ref[...] + other_ref[...].astype(jnp.float32)
    low, high = unpacked(is_heavy(own), pair[:SLOT], pair[SLOT:])
    out_ref[:SLOT, :] = jnp.where(valid[:SLOT], low, 0.0).astype(jnp.bfloat16)
    out_ref[SLOT:, :] = jnp.where(valid[SLOT:], high, 0.0).astype(jnp.bfloat16)


def shards(query_rows, key_rows, value_rows, proj_weight, out_grad, image_starts):
    dp_size, mp_size = lax.axis_size("dp"), lax.axis_size("mp")
    width = query_rows.shape[1]
    near = mp_size // 4
    far = near + 1
    dp, z = lax.axis_index("dp"), lax.axis_index("mp")
    hop_perm = ring_pairs(dp_size, mp_size, 1)
    jump_perm = ring_pairs(dp_size, mp_size, far)
    swap_perm = [(i, (i + dp_size // 2) % dp_size) for i in range(dp_size)]
    right = goes_right(dp, dp_size)
    delta = jnp.where(right, 1, mp_size - 1)
    rows_type = jax.ShapeDtypeStruct((ROWS, width), jnp.bfloat16)
    half_type = jax.ShapeDtypeStruct((ROWS + SLOT, width), jnp.bfloat16)

    def hop(rows):
        return lax.ppermute(rows, ("dp", "mp"), hop_perm)

    def jump(rows):
        return lax.ppermute(rows, ("dp", "mp"), jump_perm)

    def swap(rows):
        return lax.ppermute(rows, "dp", swap_perm)

    def half_of(rows):
        return jnp.where(right, rows[:SLOT], rows[SLOT:])

    def place_half(rows):
        zeros = jnp.zeros_like(rows)
        return jnp.concatenate([jnp.where(right, rows, zeros), jnp.where(right, zeros, rows)], 0)

    def block_of(array, index):
        return lax.dynamic_slice_in_dim(array, lax.rem(index, mp_size) * width, width, 1)

    other_out_grad = swap(out_grad)
    in_any = pl.BlockSpec(memory_space=pl.ANY)
    in_hbm = pl.BlockSpec(memory_space=pltpu.HBM)
    row_buffer = pltpu.VMEM((ROWS, width), jnp.bfloat16)
    attended, own_out_grad, held, starts = call(
        functools.partial(forward_kernel, dp_size, mp_size, (near, near + far - 1)),
        [
            rows_type,
            rows_type,
            jax.ShapeDtypeStruct((2, width, width), jnp.bfloat16),
            jax.ShapeDtypeStruct((2, ROWS), jnp.int32),
        ],
        (query_rows, key_rows, value_rows, out_grad, proj_weight, image_starts),
        specs=[in_hbm] * 6,
        scratch=[row_buffer] * 3
        + [pltpu.VMEM(image_starts.shape, jnp.int32), pltpu.SemaphoreType.DMA((7,))],
        flops=4 * ROWS * ROWS * width,
        name="attention_forward",
        limit=FRONT_LIMIT,
    )
    other_attended = swap(attended)
    (pair_grad,) = call(
        pack_kernel, [rows_type], (own_out_grad, other_out_grad, starts), name="pack_out_grad"
    )
    near_block, far_block = hop(pair_grad), jump(pair_grad)
    pair_attended, first_terms = call(
        functools.partial(pack_terms_kernel, dp_size),
        [rows_type, half_type],
        (attended, other_attended, starts, held, pair_grad),
        specs=[IN_VMEM] * 4 + [in_any],
        name="pack_attended",
    )

    def product(block, distance):
        return dot(block, block_of(proj_weight, z + distance * (mp_size - delta)), (1, 1))

    def add_terms(sums, step):
        distances = (near - step, near + far - 1 - step)
        joined = jax.ShapeDtypeStruct((2 * ROWS, width), jnp.bfloat16)
        return call(
            functools.partial(add_terms_kernel, dp_size, mp_size, distances),
            [rows_type, rows_type] if step == near - 1 else [joined],
            (sums, pair_attended, proj_weight),
            flops=4 * ROWS * width * width,
            name="add_terms",
        )

    sums = hop(first_terms)
    for step in range(1, near - 1):
        sums = hop(*add_terms(sums, step))
        if step == 1:
            (moved,) = call(
                join_kernel,
                [jax.ShapeDtypeStruct((2 * ROWS, width), jnp.bfloat16)],
                (near_block, far_block, first_terms),
                specs=[IN_VMEM] * 2 + [in_any],
                name="join_out_grad",
            )
    near_sum, last_sum = add_terms(sums, near - 1)
    last_sum, near_sum = jump(last_sum), hop(near_sum)

    partial = place_half(product(half_of(pair_grad), 0))
    for step in range(1, near):
        near_block, far_block = moved[:ROWS], moved[ROWS:]
        partial = partial + product(near_block, step) + product(far_block, far + step - 1)
        if step == near - 1:
            moved = jnp.concatenate([near_block, half_of(far_block)], 0)
        moved = hop(moved)
    near_block, far_block = moved[:ROWS], moved[ROWS:]
    partial = partial + product(near_block, near) + place_half(product(far_block, near + far - 1))
    other_partial = swap(partial.astype(jnp.bfloat16))
    last_sum, other_partial = lax.optimization_barrier((last_sum, other_partial))
    total = (
        near_sum.astype(jnp.float32)
        + last_sum.astype(jnp.float32)
        + place_half(dot(half_of(pair_attended), block_of(proj_weight, z)))
    )
    other_total = swap(total.astype(jnp.bfloat16))
    grads = call(
        backward_kernel,
        [rows_type] * 3,
        (query_rows, key_rows, value_rows, partial, other_partial, starts),
        scratch=[pltpu.VMEM((ROWS, width), jnp.bfloat16)],
        flops=12 * ROWS * ROWS * width,
        name="attention_backward",
    )
    (projected,) = call(
        finish_kernel,
        [rows_type],
        (total, other_total, starts),
        name="finish_projected",
    )
    return (projected, *grads)


def solution(mesh):
    placed = (P("dp", "mp"), P("dp", "mp"), P("dp", "mp"), P("mp", None), P("dp", "mp"), P())
    return jax.shard_map(
        shards,
        mesh=mesh,
        in_specs=placed,
        out_specs=(P("dp", "mp"), P("dp", "mp"), P("dp", "mp"), P("dp", "mp")),
        check_vma=False,
    )
```

```python
import functools
import math

import jax
import jax.numpy as jnp
from jax import lax
from jax.experimental import pallas as pl
from jax.experimental.pallas import tpu as pltpu
from jax.sharding import PartitionSpec as P

HEAD_DIM = 128
SLOT = 128
ROWS = 256
VMEM_LIMIT = 20 * 1024 * 1024
FRONT_LIMIT = 54600 * 1024
IN_VMEM = pl.BlockSpec(memory_space=pltpu.VMEM)


def ring_pairs(dp_size, mp_size, distance):
    pairs = []
    for dp in range(dp_size):
        step = distance if goes_right(dp, dp_size) else mp_size - distance
        for z in range(mp_size):
            pairs.append((dp * mp_size + z, dp * mp_size + (z + step) % mp_size))
    return pairs


def goes_right(dp, dp_size):
    half = dp_size // 2
    if isinstance(dp, int):
        return (dp // half + dp) % 2 == 0
    return lax.rem(lax.div(dp, half) + dp, 2) == 0


def dot(a, b, dims=(1, 0)):
    return lax.dot_general(
        a, b, (((dims[0],), (dims[1],)), ((), ())), preferred_element_type=jnp.float32
    )


def call(kernel, outs, operands, specs=None, scratch=(), flops=0, name=None, limit=VMEM_LIMIT):
    moved = sum(math.prod(a.shape) * a.dtype.itemsize for a in (*operands, *outs))
    return pl.pallas_call(
        kernel,
        out_shape=outs,
        in_specs=specs or [IN_VMEM] * len(operands),
        out_specs=[IN_VMEM] * len(outs),
        scratch_shapes=list(scratch),
        compiler_params=pltpu.CompilerParams(vmem_limit_bytes=limit),
        cost_estimate=pl.CostEstimate(flops=flops, bytes_accessed=moved, transcendentals=0),
        name=name,
    )(*operands)


def starts_of(starts_ref):
    return starts_ref[0:1, :], starts_ref[1:2, :]


def as_column(row):
    size = row.shape[1]
    on_diagonal = lax.broadcasted_iota(jnp.int32, (size, size), 0) == lax.broadcasted_iota(
        jnp.int32, (size, size), 1
    )
    return jnp.sum(jnp.where(on_diagonal, row, 0), axis=1, keepdims=True)


def is_heavy(own):
    lanes = lax.broadcasted_iota(jnp.int32, own.shape, 1)
    return jnp.sum(jnp.where(lanes == SLOT - 1, own, 0)) >= 0


def flip_matrix():
    total = lax.broadcasted_iota(jnp.int32, (SLOT, SLOT), 0) + lax.broadcasted_iota(
        jnp.int32, (SLOT, SLOT), 1
    )
    return jnp.where(total == SLOT - 1, 1.0, 0.0).astype(jnp.bfloat16)


def packed_slots(own_starts, other_starts, own_ref, other_ref):
    heavy = is_heavy(own_starts)
    light_starts = jnp.where(heavy, other_starts, own_starts)
    light_count = jnp.sum((light_starts >= 0).astype(jnp.int32))
    from_light = lax.broadcasted_iota(jnp.int32, (SLOT, 1), 0) < light_count
    own_first, other_first = own_ref[:SLOT, :], other_ref[:SLOT, :]
    first = jnp.where(heavy, own_first, other_first)
    light = jnp.where(heavy, other_first, own_first)
    second = jnp.where(heavy, own_ref[SLOT:, :], other_ref[SLOT:, :])
    flipped = dot(flip_matrix(), second)
    second_slot = jnp.where(from_light, light.astype(jnp.float32), flipped).astype(jnp.bfloat16)
    return first, second_slot


def pack_kernel(own_ref, other_ref, starts_ref, out_ref):
    first, second = packed_slots(*starts_of(starts_ref), own_ref, other_ref)
    out_ref[:SLOT, :] = first
    out_ref[SLOT:, :] = second


def pack_terms_kernel(
    dp_size,
    mp_size,
    distances,
    own_ref,
    other_ref,
    starts_ref,
    weight_ref,
    earlier_ref,
    out_ref,
    terms_ref,
):
    del earlier_ref
    right = goes_right(lax.axis_index("dp"), dp_size)
    first, second = packed_slots(*starts_of(starts_ref), own_ref, other_ref)
    out_ref[:SLOT, :] = first
    out_ref[SLOT:, :] = second
    half = jnp.where(right, first, second)
    near_weight, far_weight = weights_at(dp_size, mp_size, distances, weight_ref)
    terms_ref[:SLOT, :] = dot(first, near_weight).astype(jnp.bfloat16)
    terms_ref[SLOT:ROWS, :] = dot(second, near_weight).astype(jnp.bfloat16)
    terms_ref[ROWS:, :] = dot(half, far_weight).astype(jnp.bfloat16)


def weights_at(dp_size, mp_size, distances, weight_ref):
    width = weight_ref.shape[0]
    right = goes_right(lax.axis_index("dp"), dp_size)
    found = []
    for distance in distances:
        ahead = jnp.where(right, distance, mp_size - distance)
        index = lax.rem(lax.axis_index("mp") + ahead, mp_size)
        found.append(weight_ref[:, pl.ds(pl.multiple_of(index * width, 128), width)])
    return found


def add_terms_kernel(dp_size, mp_size, distances, sums_ref, rows_ref, weight_ref, *out_refs):
    near_weight, far_weight = weights_at(dp_size, mp_size, distances, weight_ref)
    near_term, far_term = dot(rows_ref[...], near_weight), dot(rows_ref[...], far_weight)
    near_sum = sums_ref[:ROWS, :].astype(jnp.float32) + near_term
    if sums_ref.shape[0] == 2 * ROWS:
        far_sum = sums_ref[ROWS:, :].astype(jnp.float32) + far_term
    else:
        right = goes_right(lax.axis_index("dp"), dp_size)
        half = sums_ref[ROWS:, :].astype(jnp.float32)
        first = jnp.where(right, half, 0.0) + far_term[:SLOT]
        second = jnp.where(right, 0.0, half) + far_term[SLOT:]
        far_sum = jnp.concatenate([first, second], 0)
    if len(out_refs) == 2:
        out_refs[0][...] = near_sum.astype(jnp.bfloat16)
        out_refs[1][...] = far_sum.astype(jnp.bfloat16)
    else:
        out_refs[0][:ROWS, :] = near_sum.astype(jnp.bfloat16)
        out_refs[0][ROWS:, :] = far_sum.astype(jnp.bfloat16)


def join_kernel(near_ref, far_ref, earlier_ref, out_ref):
    del earlier_ref
    out_ref[:ROWS, :] = near_ref[...]
    out_ref[ROWS:, :] = far_ref[...]


def probabilities_of(query, key, same_image):
    scores = dot(query, key, (1, 1)) / math.sqrt(HEAD_DIM)
    scores = jnp.where(same_image, scores, -jnp.inf)
    weights = jnp.exp(scores - jnp.max(scores, axis=1, keepdims=True))
    return weights * (1.0 / jnp.sum(weights, axis=1, keepdims=True))


def forward_kernel(
    dp_size,
    query_hbm,
    key_hbm,
    value_hbm,
    out_grad_hbm,
    starts_hbm,
    out_ref,
    out_grad_ref,
    pair_starts_ref,
    query_ref,
    key_ref,
    value_ref,
    starts_ref,
    sems,
):
    width = query_ref.shape[1]
    dp = lax.axis_index("dp")
    moves = [
        (starts_hbm, starts_ref),
        (query_hbm, query_ref),
        (key_hbm, key_ref),
        (value_hbm, value_ref),
        (out_grad_hbm, out_grad_ref),
    ]
    copies = [pltpu.make_async_copy(*move, sems.at[at]) for at, move in enumerate(moves)]
    for copy in copies:
        copy.start()
    copies[0].wait()
    own = starts_ref[pl.ds(dp, 1), :]
    pair_starts_ref[0:1, :] = own
    pair_starts_ref[1:2, :] = starts_ref[pl.ds(lax.rem(dp + dp_size // 2, dp_size), 1), :]
    for copy in copies[1:4]:
        copy.wait()
    same_image = as_column(own) == own
    for head in range(width // HEAD_DIM):
        at = slice(head * HEAD_DIM, (head + 1) * HEAD_DIM)
        rounded = probabilities_of(query_ref[:, at], key_ref[:, at], same_image).astype(jnp.bfloat16)
        out_ref[:, at] = dot(rounded, value_ref[:, at]).astype(jnp.bfloat16)
    for copy in copies[4:]:
        copy.wait()


def unpacked(heavy, first, second):
    own_first = jnp.where(heavy, first, second)
    return own_first, dot(flip_matrix(), second.astype(jnp.bfloat16))


def backward_kernel(
    query_ref,
    key_ref,
    value_ref,
    partial_ref,
    other_ref,
    starts_ref,
    grad_query_ref,
    grad_key_ref,
    grad_value_ref,
    grad_ref,
):
    own, _ = starts_of(starts_ref)
    column = as_column(own)
    same_image = column == own
    valid = column >= 0
    pair = partial_ref[...] + other_ref[...].astype(jnp.float32)
    low, high = unpacked(is_heavy(own), pair[:SLOT], pair[SLOT:])
    grad_ref[:SLOT, :] = low.astype(jnp.bfloat16)
    grad_ref[SLOT:, :] = high.astype(jnp.bfloat16)
    for head in range(query_ref.shape[1] // HEAD_DIM):
        at = slice(head * HEAD_DIM, (head + 1) * HEAD_DIM)
        query, key, value, grad = query_ref[:, at], key_ref[:, at], value_ref[:, at], grad_ref[:, at]
        probabilities = probabilities_of(query, key, same_image)
        rounded = probabilities.astype(jnp.bfloat16)
        grad_value = dot(rounded, grad, (0, 0))
        grad_weights = dot(grad, value, (1, 1))
        correction = jnp.sum(probabilities * grad_weights, axis=1, keepdims=True)
        grad_scores = (probabilities * (grad_weights - correction) / math.sqrt(HEAD_DIM)).astype(
            jnp.bfloat16
        )
        grad_query = dot(grad_scores, key)
        grad_key = dot(grad_scores, query, (0, 0))
        grad_query_ref[:, at] = jnp.where(valid, grad_query, 0.0).astype(jnp.bfloat16)
        grad_key_ref[:, at] = jnp.where(valid, grad_key, 0.0).astype(jnp.bfloat16)
        grad_value_ref[:, at] = jnp.where(valid, grad_value, 0.0).astype(jnp.bfloat16)


def finish_kernel(total_ref, other_ref, starts_ref, out_ref):
    own, _ = starts_of(starts_ref)
    valid = as_column(own) >= 0
    pair = total_ref[...] + other_ref[...].astype(jnp.float32)
    low, high = unpacked(is_heavy(own), pair[:SLOT], pair[SLOT:])
    out_ref[:SLOT, :] = jnp.where(valid[:SLOT], low, 0.0).astype(jnp.bfloat16)
    out_ref[SLOT:, :] = jnp.where(valid[SLOT:], high, 0.0).astype(jnp.bfloat16)


def shards(query_rows, key_rows, value_rows, proj_weight, out_grad, image_starts):
    dp_size, mp_size = lax.axis_size("dp"), lax.axis_size("mp")
    width = query_rows.shape[1]
    near = mp_size // 4
    far = near + 1
    dp, z = lax.axis_index("dp"), lax.axis_index("mp")
    hop_perm = ring_pairs(dp_size, mp_size, 1)
    jump_perm = ring_pairs(dp_size, mp_size, far)
    swap_perm = [(i, (i + dp_size // 2) % dp_size) for i in range(dp_size)]
    right = goes_right(dp, dp_size)
    delta = jnp.where(right, 1, mp_size - 1)
    rows_type = jax.ShapeDtypeStruct((ROWS, width), jnp.bfloat16)
    half_type = jax.ShapeDtypeStruct((ROWS + SLOT, width), jnp.bfloat16)

    def hop(rows):
        return lax.ppermute(rows, ("dp", "mp"), hop_perm)

    def jump(rows):
        return lax.ppermute(rows, ("dp", "mp"), jump_perm)

    def swap(rows):
        return lax.ppermute(rows, "dp", swap_perm)

    def half_of(rows):
        return jnp.where(right, rows[:SLOT], rows[SLOT:])

    def place_half(rows):
        zeros = jnp.zeros_like(rows)
        return jnp.concatenate([jnp.where(right, rows, zeros), jnp.where(right, zeros, rows)], 0)

    def block_of(array, index):
        return lax.dynamic_slice_in_dim(array, lax.rem(index, mp_size) * width, width, 1)

    other_out_grad = swap(out_grad)
    in_any = pl.BlockSpec(memory_space=pl.ANY)
    in_hbm = pl.BlockSpec(memory_space=pltpu.HBM)
    row_buffer = pltpu.VMEM((ROWS, width), jnp.bfloat16)
    attended, own_out_grad, starts = call(
        functools.partial(forward_kernel, dp_size),
        [
            rows_type,
            rows_type,
            jax.ShapeDtypeStruct((2, ROWS), jnp.int32),
        ],
        (query_rows, key_rows, value_rows, out_grad, image_starts),
        specs=[in_hbm] * 5,
        scratch=[row_buffer] * 3
        + [pltpu.VMEM(image_starts.shape, jnp.int32), pltpu.SemaphoreType.DMA((5,))],
        flops=4 * ROWS * ROWS * width,
        name="attention_forward",
        limit=FRONT_LIMIT,
    )
    other_attended = swap(attended)
    (pair_grad,) = call(
        pack_kernel, [rows_type], (own_out_grad, other_out_grad, starts), name="pack_out_grad"
    )
    near_block, far_block = hop(pair_grad), jump(pair_grad)
    pair_attended, first_terms = call(
        functools.partial(pack_terms_kernel, dp_size, mp_size, (near, near + far - 1)),
        [rows_type, half_type],
        (attended, other_attended, starts, proj_weight, pair_grad),
        specs=[IN_VMEM] * 4 + [in_any],
        name="pack_attended",
    )

    def product(block, distance):
        return dot(block, block_of(proj_weight, z + distance * (mp_size - delta)), (1, 1))

    def add_terms(sums, step):
        distances = (near - step, near + far - 1 - step)
        joined = jax.ShapeDtypeStruct((2 * ROWS, width), jnp.bfloat16)
        return call(
            functools.partial(add_terms_kernel, dp_size, mp_size, distances),
            [rows_type, rows_type] if step == near - 1 else [joined],
            (sums, pair_attended, proj_weight),
            flops=4 * ROWS * width * width,
            name="add_terms",
        )

    sums = hop(first_terms)
    for step in range(1, near - 1):
        sums = hop(*add_terms(sums, step))
        if step == 1:
            (moved,) = call(
                join_kernel,
                [jax.ShapeDtypeStruct((2 * ROWS, width), jnp.bfloat16)],
                (near_block, far_block, first_terms),
                specs=[IN_VMEM] * 2 + [in_any],
                name="join_out_grad",
            )
    near_sum, last_sum = add_terms(sums, near - 1)
    last_sum, near_sum = jump(last_sum), hop(near_sum)

    partial = place_half(product(half_of(pair_grad), 0))
    for step in range(1, near):
        near_block, far_block = moved[:ROWS], moved[ROWS:]
        partial = partial + product(near_block, step) + product(far_block, far + step - 1)
        if step == near - 1:
            moved = jnp.concatenate([near_block, half_of(far_block)], 0)
        moved = hop(moved)
    near_block, far_block = moved[:ROWS], moved[ROWS:]
    partial = partial + product(near_block, near) + place_half(product(far_block, near + far - 1))
    other_partial = swap(partial.astype(jnp.bfloat16))
    last_sum, other_partial = lax.optimization_barrier((last_sum, other_partial))
    total = (
        near_sum.astype(jnp.float32)
        + last_sum.astype(jnp.float32)
        + place_half(dot(half_of(pair_attended), block_of(proj_weight, z)))
    )
    other_total = swap(total.astype(jnp.bfloat16))
    grads = call(
        backward_kernel,
        [rows_type] * 3,
        (query_rows, key_rows, value_rows, partial, other_partial, starts),
        scratch=[pltpu.VMEM((ROWS, width), jnp.bfloat16)],
        flops=12 * ROWS * ROWS * width,
        name="attention_backward",
    )
    (projected,) = call(
        finish_kernel,
        [rows_type],
        (total, other_total, starts),
        name="finish_projected",
    )
    return (projected, *grads)


def solution(mesh):
    placed = (P("dp", "mp"), P("dp", "mp"), P("dp", "mp"), P("mp", None), P("dp", "mp"), P())
    return jax.shard_map(
        shards,
        mesh=mesh,
        in_specs=placed,
        out_specs=(P("dp", "mp"), P("dp", "mp"), P("dp", "mp"), P("dp", "mp")),
        check_vma=False,
    )
```

```python
import functools
import math

import jax
import jax.numpy as jnp
from jax import lax
from jax.experimental import pallas as pl
from jax.experimental.pallas import tpu as pltpu
from jax.sharding import PartitionSpec as P

HEAD_DIM = 128
SLOT = 128
ROWS = 256
VMEM_LIMIT = 20 * 1024 * 1024
FRONT_LIMIT = 54600 * 1024
IN_VMEM = pl.BlockSpec(memory_space=pltpu.VMEM)


def ring_pairs(dp_size, mp_size, distance):
    pairs = []
    for dp in range(dp_size):
        step = distance if goes_right(dp, dp_size) else mp_size - distance
        for z in range(mp_size):
            pairs.append((dp * mp_size + z, dp * mp_size + (z + step) % mp_size))
    return pairs


def goes_right(dp, dp_size):
    half = dp_size // 2
    if isinstance(dp, int):
        return (dp // half + dp) % 2 == 0
    return lax.rem(lax.div(dp, half) + dp, 2) == 0


def dot(a, b, dims=(1, 0)):
    return lax.dot_general(
        a, b, (((dims[0],), (dims[1],)), ((), ())), preferred_element_type=jnp.float32
    )


def call(kernel, outs, operands, specs=None, scratch=(), flops=0, name=None, limit=VMEM_LIMIT):
    moved = sum(math.prod(a.shape) * a.dtype.itemsize for a in (*operands, *outs))
    return pl.pallas_call(
        kernel,
        out_shape=outs,
        in_specs=specs or [IN_VMEM] * len(operands),
        out_specs=[IN_VMEM] * len(outs),
        scratch_shapes=list(scratch),
        compiler_params=pltpu.CompilerParams(vmem_limit_bytes=limit),
        cost_estimate=pl.CostEstimate(flops=flops, bytes_accessed=moved, transcendentals=0),
        name=name,
    )(*operands)


def starts_of(starts_ref):
    return starts_ref[0:1, :], starts_ref[1:2, :]


def as_column(row):
    size = row.shape[1]
    on_diagonal = lax.broadcasted_iota(jnp.int32, (size, size), 0) == lax.broadcasted_iota(
        jnp.int32, (size, size), 1
    )
    return jnp.sum(jnp.where(on_diagonal, row, 0), axis=1, keepdims=True)


def is_heavy(own):
    lanes = lax.broadcasted_iota(jnp.int32, own.shape, 1)
    return jnp.sum(jnp.where(lanes == SLOT - 1, own, 0)) >= 0


def flip_matrix():
    total = lax.broadcasted_iota(jnp.int32, (SLOT, SLOT), 0) + lax.broadcasted_iota(
        jnp.int32, (SLOT, SLOT), 1
    )
    return jnp.where(total == SLOT - 1, 1.0, 0.0).astype(jnp.bfloat16)


def packed_slots(own_starts, other_starts, own_ref, other_ref):
    heavy = is_heavy(own_starts)
    light_starts = jnp.where(heavy, other_starts, own_starts)
    light_count = jnp.sum((light_starts >= 0).astype(jnp.int32))
    from_light = lax.broadcasted_iota(jnp.int32, (SLOT, 1), 0) < light_count
    own_first, other_first = own_ref[:SLOT, :], other_ref[:SLOT, :]
    first = jnp.where(heavy, own_first, other_first)
    light = jnp.where(heavy, other_first, own_first)
    second = jnp.where(heavy, own_ref[SLOT:, :], other_ref[SLOT:, :])
    flipped = dot(flip_matrix(), second)
    second_slot = jnp.where(from_light, light.astype(jnp.float32), flipped).astype(jnp.bfloat16)
    return first, second_slot


def pack_kernel(own_ref, other_ref, starts_ref, out_ref):
    first, second = packed_slots(*starts_of(starts_ref), own_ref, other_ref)
    out_ref[:SLOT, :] = first
    out_ref[SLOT:, :] = second


def pack_terms_kernel(
    dp_size,
    mp_size,
    distances,
    own_ref,
    other_ref,
    starts_ref,
    weight_ref,
    earlier_ref,
    out_ref,
    terms_ref,
):
    del earlier_ref
    right = goes_right(lax.axis_index("dp"), dp_size)
    first, second = packed_slots(*starts_of(starts_ref), own_ref, other_ref)
    out_ref[:SLOT, :] = first
    out_ref[SLOT:, :] = second
    half = jnp.where(right, first, second)
    near_weight, far_weight = weights_at(dp_size, mp_size, distances, weight_ref)
    terms_ref[:SLOT, :] = dot(first, near_weight).astype(jnp.bfloat16)
    terms_ref[SLOT:ROWS, :] = dot(second, near_weight).astype(jnp.bfloat16)
    terms_ref[ROWS:, :] = dot(half, far_weight).astype(jnp.bfloat16)


def weights_at(dp_size, mp_size, distances, weight_ref):
    width = weight_ref.shape[0]
    right = goes_right(lax.axis_index("dp"), dp_size)
    found = []
    for distance in distances:
        ahead = jnp.where(right, distance, mp_size - distance)
        index = lax.rem(lax.axis_index("mp") + ahead, mp_size)
        found.append(weight_ref[:, pl.ds(pl.multiple_of(index * width, 128), width)])
    return found


def add_terms_kernel(dp_size, mp_size, distances, sums_ref, rows_ref, weight_ref, *out_refs):
    near_weight, far_weight = weights_at(dp_size, mp_size, distances, weight_ref)
    near_term, far_term = dot(rows_ref[...], near_weight), dot(rows_ref[...], far_weight)
    near_sum = sums_ref[:ROWS, :].astype(jnp.float32) + near_term
    if sums_ref.shape[0] == 2 * ROWS:
        far_sum = sums_ref[ROWS:, :].astype(jnp.float32) + far_term
    else:
        right = goes_right(lax.axis_index("dp"), dp_size)
        half = sums_ref[ROWS:, :].astype(jnp.float32)
        first = jnp.where(right, half, 0.0) + far_term[:SLOT]
        second = jnp.where(right, 0.0, half) + far_term[SLOT:]
        far_sum = jnp.concatenate([first, second], 0)
    if len(out_refs) == 2:
        out_refs[0][...] = near_sum.astype(jnp.bfloat16)
        out_refs[1][...] = far_sum.astype(jnp.bfloat16)
    else:
        out_refs[0][:ROWS, :] = near_sum.astype(jnp.bfloat16)
        out_refs[0][ROWS:, :] = far_sum.astype(jnp.bfloat16)


def total_kernel(
    dp_size,
    mp_size,
    near_ref,
    last_ref,
    rows_ref,
    weight_ref,
    earlier_ref,
    total_ref,
    sent_ref,
):
    del earlier_ref
    right = goes_right(lax.axis_index("dp"), dp_size)
    (weight,) = weights_at(dp_size, mp_size, (0,), weight_ref)
    own = dot(jnp.where(right, rows_ref[:SLOT, :], rows_ref[SLOT:, :]), weight)
    total = near_ref[...].astype(jnp.float32) + last_ref[...].astype(jnp.float32)
    total_ref[:SLOT, :] = total[:SLOT] + jnp.where(right, own, 0.0)
    total_ref[SLOT:, :] = total[SLOT:] + jnp.where(right, 0.0, own)
    sent_ref[...] = total_ref[...].astype(jnp.bfloat16)


def join_kernel(near_ref, far_ref, earlier_ref, out_ref):
    del earlier_ref
    out_ref[:ROWS, :] = near_ref[...]
    out_ref[ROWS:, :] = far_ref[...]


def probabilities_of(query, key, same_image):
    scores = dot(query, key, (1, 1)) / math.sqrt(HEAD_DIM)
    scores = jnp.where(same_image, scores, -jnp.inf)
    weights = jnp.exp(scores - jnp.max(scores, axis=1, keepdims=True))
    return weights * (1.0 / jnp.sum(weights, axis=1, keepdims=True))


def forward_kernel(
    dp_size,
    query_hbm,
    key_hbm,
    value_hbm,
    out_grad_hbm,
    starts_hbm,
    out_ref,
    out_grad_ref,
    pair_starts_ref,
    query_ref,
    key_ref,
    value_ref,
    starts_ref,
    sems,
):
    width = query_ref.shape[1]
    dp = lax.axis_index("dp")
    moves = [
        (starts_hbm, starts_ref),
        (query_hbm, query_ref),
        (key_hbm, key_ref),
        (value_hbm, value_ref),
        (out_grad_hbm, out_grad_ref),
    ]
    copies = [pltpu.make_async_copy(*move, sems.at[at]) for at, move in enumerate(moves)]
    for copy in copies:
        copy.start()
    copies[0].wait()
    own = starts_ref[pl.ds(dp, 1), :]
    pair_starts_ref[0:1, :] = own
    pair_starts_ref[1:2, :] = starts_ref[pl.ds(lax.rem(dp + dp_size // 2, dp_size), 1), :]
    for copy in copies[1:4]:
        copy.wait()
    same_image = as_column(own) == own
    for head in range(width // HEAD_DIM):
        at = slice(head * HEAD_DIM, (head + 1) * HEAD_DIM)
        rounded = probabilities_of(query_ref[:, at], key_ref[:, at], same_image).astype(jnp.bfloat16)
        out_ref[:, at] = dot(rounded, value_ref[:, at]).astype(jnp.bfloat16)
    for copy in copies[4:]:
        copy.wait()


def unpacked(heavy, first, second):
    own_first = jnp.where(heavy, first, second)
    return own_first, dot(flip_matrix(), second.astype(jnp.bfloat16))


def backward_kernel(
    query_ref,
    key_ref,
    value_ref,
    partial_ref,
    other_ref,
    starts_ref,
    grad_query_ref,
    grad_key_ref,
    grad_value_ref,
    grad_ref,
):
    own, _ = starts_of(starts_ref)
    column = as_column(own)
    same_image = column == own
    valid = column >= 0
    pair = partial_ref[...] + other_ref[...].astype(jnp.float32)
    low, high = unpacked(is_heavy(own), pair[:SLOT], pair[SLOT:])
    grad_ref[:SLOT, :] = low.astype(jnp.bfloat16)
    grad_ref[SLOT:, :] = high.astype(jnp.bfloat16)
    for head in range(query_ref.shape[1] // HEAD_DIM):
        at = slice(head * HEAD_DIM, (head + 1) * HEAD_DIM)
        query, key, value, grad = query_ref[:, at], key_ref[:, at], value_ref[:, at], grad_ref[:, at]
        probabilities = probabilities_of(query, key, same_image)
        rounded = probabilities.astype(jnp.bfloat16)
        grad_value = dot(rounded, grad, (0, 0))
        grad_weights = dot(grad, value, (1, 1))
        correction = jnp.sum(probabilities * grad_weights, axis=1, keepdims=True)
        grad_scores = (probabilities * (grad_weights - correction) / math.sqrt(HEAD_DIM)).astype(
            jnp.bfloat16
        )
        grad_query = dot(grad_scores, key)
        grad_key = dot(grad_scores, query, (0, 0))
        grad_query_ref[:, at] = jnp.where(valid, grad_query, 0.0).astype(jnp.bfloat16)
        grad_key_ref[:, at] = jnp.where(valid, grad_key, 0.0).astype(jnp.bfloat16)
        grad_value_ref[:, at] = jnp.where(valid, grad_value, 0.0).astype(jnp.bfloat16)


def finish_kernel(total_ref, other_ref, starts_ref, out_ref):
    own, _ = starts_of(starts_ref)
    valid = as_column(own) >= 0
    pair = total_ref[...] + other_ref[...].astype(jnp.float32)
    low, high = unpacked(is_heavy(own), pair[:SLOT], pair[SLOT:])
    out_ref[:SLOT, :] = jnp.where(valid[:SLOT], low, 0.0).astype(jnp.bfloat16)
    out_ref[SLOT:, :] = jnp.where(valid[SLOT:], high, 0.0).astype(jnp.bfloat16)


def shards(query_rows, key_rows, value_rows, proj_weight, out_grad, image_starts):
    dp_size, mp_size = lax.axis_size("dp"), lax.axis_size("mp")
    width = query_rows.shape[1]
    near = mp_size // 4
    far = near + 1
    dp, z = lax.axis_index("dp"), lax.axis_index("mp")
    hop_perm = ring_pairs(dp_size, mp_size, 1)
    jump_perm = ring_pairs(dp_size, mp_size, far)
    gather_perm = ring_pairs(dp_size, mp_size, near)
    swap_perm = [(i, (i + dp_size // 2) % dp_size) for i in range(dp_size)]
    right = goes_right(dp, dp_size)
    delta = jnp.where(right, 1, mp_size - 1)
    rows_type = jax.ShapeDtypeStruct((ROWS, width), jnp.bfloat16)
    half_type = jax.ShapeDtypeStruct((ROWS + SLOT, width), jnp.bfloat16)

    def hop(rows):
        return lax.ppermute(rows, ("dp", "mp"), hop_perm)

    def jump(rows):
        return lax.ppermute(rows, ("dp", "mp"), jump_perm)

    def swap(rows):
        return lax.ppermute(rows, "dp", swap_perm)

    def half_of(rows):
        return jnp.where(right, rows[:SLOT], rows[SLOT:])

    def place_half(rows):
        zeros = jnp.zeros_like(rows)
        return jnp.concatenate([jnp.where(right, rows, zeros), jnp.where(right, zeros, rows)], 0)

    def block_of(array, index):
        return lax.dynamic_slice_in_dim(array, lax.rem(index, mp_size) * width, width, 1)

    other_out_grad = swap(out_grad)
    in_any = pl.BlockSpec(memory_space=pl.ANY)
    in_hbm = pl.BlockSpec(memory_space=pltpu.HBM)
    row_buffer = pltpu.VMEM((ROWS, width), jnp.bfloat16)
    attended, own_out_grad, starts = call(
        functools.partial(forward_kernel, dp_size),
        [
            rows_type,
            rows_type,
            jax.ShapeDtypeStruct((2, ROWS), jnp.int32),
        ],
        (query_rows, key_rows, value_rows, out_grad, image_starts),
        specs=[in_hbm] * 5,
        scratch=[row_buffer] * 3
        + [pltpu.VMEM(image_starts.shape, jnp.int32), pltpu.SemaphoreType.DMA((5,))],
        flops=4 * ROWS * ROWS * width,
        name="attention_forward",
        limit=FRONT_LIMIT,
    )
    other_attended = swap(attended)
    (pair_grad,) = call(
        pack_kernel, [rows_type], (own_out_grad, other_out_grad, starts), name="pack_out_grad"
    )
    near_block = hop(pair_grad)
    far_block = lax.ppermute(pair_grad, ("dp", "mp"), gather_perm)
    pair_attended, first_terms = call(
        functools.partial(pack_terms_kernel, dp_size, mp_size, (near, near + far - 1)),
        [rows_type, half_type],
        (attended, other_attended, starts, proj_weight, pair_grad),
        specs=[IN_VMEM] * 4 + [in_any],
        name="pack_attended",
    )

    def product(block, distance):
        return dot(block, block_of(proj_weight, z + distance * (mp_size - delta)), (1, 1))

    def add_terms(sums, step):
        distances = (near - step, near + far - 1 - step)
        joined = jax.ShapeDtypeStruct((2 * ROWS, width), jnp.bfloat16)
        return call(
            functools.partial(add_terms_kernel, dp_size, mp_size, distances),
            [rows_type, rows_type] if step == near - 1 else [joined],
            (sums, pair_attended, proj_weight),
            flops=4 * ROWS * width * width,
            name="add_terms",
        )

    sums = hop(first_terms)
    for step in range(1, near - 1):
        sums = hop(*add_terms(sums, step))
        if step == 1:
            (moved,) = call(
                join_kernel,
                [jax.ShapeDtypeStruct((2 * ROWS, width), jnp.bfloat16)],
                (near_block, far_block, first_terms),
                specs=[IN_VMEM] * 2 + [in_any],
                name="join_out_grad",
            )
    near_sum, last_sum = add_terms(sums, near - 1)
    last_sum, near_sum = jump(last_sum), hop(near_sum)

    partial = place_half(product(half_of(pair_grad), 0))
    for step in range(1, near):
        near_block, far_block = moved[:ROWS], moved[ROWS:]
        partial = partial + product(near_block, step) + product(far_block, near + step - 1)
        if step < near - 1:
            moved = hop(moved)
    far_block = hop(far_block)
    partial = partial + product(far_block, 2 * near - 1)
    far_block = hop(half_of(far_block))
    partial = partial + place_half(product(far_block, 2 * near))
    other_partial = swap(partial.astype(jnp.bfloat16))
    total, sent = call(
        functools.partial(total_kernel, dp_size, mp_size),
        [jax.ShapeDtypeStruct((ROWS, width), jnp.float32), rows_type],
        (near_sum, last_sum, pair_attended, proj_weight, partial),
        specs=[IN_VMEM] * 4 + [in_any],
        flops=2 * SLOT * width * width,
        name="total",
    )
    other_total = swap(sent)
    grads = call(
        backward_kernel,
        [rows_type] * 3,
        (query_rows, key_rows, value_rows, partial, other_partial, starts),
        scratch=[pltpu.VMEM((ROWS, width), jnp.bfloat16)],
        flops=12 * ROWS * ROWS * width,
        name="attention_backward",
    )
    (projected,) = call(
        finish_kernel,
        [rows_type],
        (total, other_total, starts),
        name="finish_projected",
    )
    return (projected, *grads)


def solution(mesh):
    placed = (P("dp", "mp"), P("dp", "mp"), P("dp", "mp"), P("mp", None), P("dp", "mp"), P())
    return jax.shard_map(
        shards,
        mesh=mesh,
        in_specs=placed,
        out_specs=(P("dp", "mp"), P("dp", "mp"), P("dp", "mp"), P("dp", "mp")),
        check_vma=False,
    )
```

```python
import functools
import math

import jax
import jax.numpy as jnp
from jax import lax
from jax.experimental import pallas as pl
from jax.experimental.pallas import tpu as pltpu
from jax.sharding import PartitionSpec as P

HEAD_DIM = 128
SLOT = 128
ROWS = 256
VMEM_LIMIT = 20 * 1024 * 1024
FRONT_LIMIT = 54600 * 1024
IN_VMEM = pl.BlockSpec(memory_space=pltpu.VMEM)


def ring_pairs(dp_size, mp_size, distance):
    pairs = []
    for dp in range(dp_size):
        step = distance if goes_right(dp, dp_size) else mp_size - distance
        for z in range(mp_size):
            pairs.append((dp * mp_size + z, dp * mp_size + (z + step) % mp_size))
    return pairs


def goes_right(dp, dp_size):
    half = dp_size // 2
    if isinstance(dp, int):
        return (dp // half + dp) % 2 == 0
    return lax.rem(lax.div(dp, half) + dp, 2) == 0


def dot(a, b, dims=(1, 0)):
    return lax.dot_general(
        a, b, (((dims[0],), (dims[1],)), ((), ())), preferred_element_type=jnp.float32
    )


def call(kernel, outs, operands, specs=None, scratch=(), flops=0, name=None, limit=VMEM_LIMIT):
    moved = sum(math.prod(a.shape) * a.dtype.itemsize for a in (*operands, *outs))
    return pl.pallas_call(
        kernel,
        out_shape=outs,
        in_specs=specs or [IN_VMEM] * len(operands),
        out_specs=[IN_VMEM] * len(outs),
        scratch_shapes=list(scratch),
        compiler_params=pltpu.CompilerParams(vmem_limit_bytes=limit),
        cost_estimate=pl.CostEstimate(flops=flops, bytes_accessed=moved, transcendentals=0),
        name=name,
    )(*operands)


def starts_of(starts_ref):
    return starts_ref[0:1, :], starts_ref[1:2, :]


def as_column(row):
    size = row.shape[1]
    on_diagonal = lax.broadcasted_iota(jnp.int32, (size, size), 0) == lax.broadcasted_iota(
        jnp.int32, (size, size), 1
    )
    return jnp.sum(jnp.where(on_diagonal, row, 0), axis=1, keepdims=True)


def is_heavy(own):
    lanes = lax.broadcasted_iota(jnp.int32, own.shape, 1)
    return jnp.sum(jnp.where(lanes == SLOT - 1, own, 0)) >= 0


def flip_matrix():
    total = lax.broadcasted_iota(jnp.int32, (SLOT, SLOT), 0) + lax.broadcasted_iota(
        jnp.int32, (SLOT, SLOT), 1
    )
    return jnp.where(total == SLOT - 1, 1.0, 0.0).astype(jnp.bfloat16)


def packed_slots(own_starts, other_starts, own_ref, other_ref):
    heavy = is_heavy(own_starts)
    light_starts = jnp.where(heavy, other_starts, own_starts)
    light_count = jnp.sum((light_starts >= 0).astype(jnp.int32))
    from_light = lax.broadcasted_iota(jnp.int32, (SLOT, 1), 0) < light_count
    own_first, other_first = own_ref[:SLOT, :], other_ref[:SLOT, :]
    first = jnp.where(heavy, own_first, other_first)
    light = jnp.where(heavy, other_first, own_first)
    second = jnp.where(heavy, own_ref[SLOT:, :], other_ref[SLOT:, :])
    flipped = dot(flip_matrix(), second)
    second_slot = jnp.where(from_light, light.astype(jnp.float32), flipped).astype(jnp.bfloat16)
    return first, second_slot


def pack_kernel(own_ref, other_ref, starts_ref, out_ref):
    first, second = packed_slots(*starts_of(starts_ref), own_ref, other_ref)
    out_ref[:SLOT, :] = first
    out_ref[SLOT:, :] = second


def pack_terms_kernel(
    dp_size,
    mp_size,
    distances,
    own_ref,
    other_ref,
    starts_ref,
    weight_ref,
    earlier_ref,
    out_ref,
    terms_ref,
):
    del earlier_ref
    right = goes_right(lax.axis_index("dp"), dp_size)
    first, second = packed_slots(*starts_of(starts_ref), own_ref, other_ref)
    out_ref[:SLOT, :] = first
    out_ref[SLOT:, :] = second
    half = jnp.where(right, first, second)
    near_weight, far_weight = weights_at(dp_size, mp_size, distances, weight_ref)
    terms_ref[:SLOT, :] = dot(first, near_weight).astype(jnp.bfloat16)
    terms_ref[SLOT:ROWS, :] = dot(second, near_weight).astype(jnp.bfloat16)
    terms_ref[ROWS:, :] = dot(half, far_weight).astype(jnp.bfloat16)


def weights_at(dp_size, mp_size, distances, weight_ref):
    width = weight_ref.shape[0]
    right = goes_right(lax.axis_index("dp"), dp_size)
    found = []
    for distance in distances:
        ahead = jnp.where(right, distance, mp_size - distance)
        index = lax.rem(lax.axis_index("mp") + ahead, mp_size)
        found.append(weight_ref[:, pl.ds(pl.multiple_of(index * width, 128), width)])
    return found


def add_terms_kernel(dp_size, mp_size, distances, sums_ref, rows_ref, weight_ref, *out_refs):
    near_weight, far_weight = weights_at(dp_size, mp_size, distances, weight_ref)
    near_term, far_term = dot(rows_ref[...], near_weight), dot(rows_ref[...], far_weight)
    near_sum = sums_ref[:ROWS, :].astype(jnp.float32) + near_term
    if sums_ref.shape[0] == 2 * ROWS:
        far_sum = sums_ref[ROWS:, :].astype(jnp.float32) + far_term
    else:
        right = goes_right(lax.axis_index("dp"), dp_size)
        half = sums_ref[ROWS:, :].astype(jnp.float32)
        first = jnp.where(right, half, 0.0) + far_term[:SLOT]
        second = jnp.where(right, 0.0, half) + far_term[SLOT:]
        far_sum = jnp.concatenate([first, second], 0)
    if len(out_refs) == 2:
        out_refs[0][...] = near_sum.astype(jnp.bfloat16)
        out_refs[1][...] = far_sum.astype(jnp.bfloat16)
    else:
        out_refs[0][:ROWS, :] = near_sum.astype(jnp.bfloat16)
        out_refs[0][ROWS:, :] = far_sum.astype(jnp.bfloat16)


def join_kernel(far_ref, near_ref, earlier_ref, out_ref):
    del earlier_ref
    out_ref[:ROWS, :] = near_ref[...]
    out_ref[ROWS:, :] = far_ref[...]


def probabilities_of(query, key, same_image):
    scores = dot(query, key, (1, 1)) / math.sqrt(HEAD_DIM)
    scores = jnp.where(same_image, scores, -jnp.inf)
    weights = jnp.exp(scores - jnp.max(scores, axis=1, keepdims=True))
    return weights * (1.0 / jnp.sum(weights, axis=1, keepdims=True))


def forward_kernel(
    dp_size,
    query_hbm,
    key_hbm,
    value_hbm,
    out_grad_hbm,
    starts_hbm,
    out_ref,
    out_grad_ref,
    pair_starts_ref,
    query_ref,
    key_ref,
    value_ref,
    starts_ref,
    sems,
):
    width = query_ref.shape[1]
    dp = lax.axis_index("dp")
    moves = [
        (starts_hbm, starts_ref),
        (query_hbm, query_ref),
        (key_hbm, key_ref),
        (value_hbm, value_ref),
        (out_grad_hbm, out_grad_ref),
    ]
    copies = [pltpu.make_async_copy(*move, sems.at[at]) for at, move in enumerate(moves)]
    for copy in copies:
        copy.start()
    copies[0].wait()
    own = starts_ref[pl.ds(dp, 1), :]
    pair_starts_ref[0:1, :] = own
    pair_starts_ref[1:2, :] = starts_ref[pl.ds(lax.rem(dp + dp_size // 2, dp_size), 1), :]
    for copy in copies[1:4]:
        copy.wait()
    same_image = as_column(own) == own
    for head in range(width // HEAD_DIM):
        at = slice(head * HEAD_DIM, (head + 1) * HEAD_DIM)
        rounded = probabilities_of(query_ref[:, at], key_ref[:, at], same_image).astype(jnp.bfloat16)
        out_ref[:, at] = dot(rounded, value_ref[:, at]).astype(jnp.bfloat16)
    for copy in copies[4:]:
        copy.wait()


def unpacked(heavy, first, second):
    own_first = jnp.where(heavy, first, second)
    return own_first, dot(flip_matrix(), second.astype(jnp.bfloat16))


def backward_kernel(
    query_ref,
    key_ref,
    value_ref,
    partial_ref,
    other_ref,
    starts_ref,
    grad_query_ref,
    grad_key_ref,
    grad_value_ref,
    grad_ref,
):
    own, _ = starts_of(starts_ref)
    column = as_column(own)
    same_image = column == own
    valid = column >= 0
    pair = partial_ref[...] + other_ref[...].astype(jnp.float32)
    low, high = unpacked(is_heavy(own), pair[:SLOT], pair[SLOT:])
    grad_ref[:SLOT, :] = low.astype(jnp.bfloat16)
    grad_ref[SLOT:, :] = high.astype(jnp.bfloat16)
    for head in range(query_ref.shape[1] // HEAD_DIM):
        at = slice(head * HEAD_DIM, (head + 1) * HEAD_DIM)
        query, key, value, grad = query_ref[:, at], key_ref[:, at], value_ref[:, at], grad_ref[:, at]
        probabilities = probabilities_of(query, key, same_image)
        rounded = probabilities.astype(jnp.bfloat16)
        grad_value = dot(rounded, grad, (0, 0))
        grad_weights = dot(grad, value, (1, 1))
        correction = jnp.sum(probabilities * grad_weights, axis=1, keepdims=True)
        grad_scores = (probabilities * (grad_weights - correction) / math.sqrt(HEAD_DIM)).astype(
            jnp.bfloat16
        )
        grad_query = dot(grad_scores, key)
        grad_key = dot(grad_scores, query, (0, 0))
        grad_query_ref[:, at] = jnp.where(valid, grad_query, 0.0).astype(jnp.bfloat16)
        grad_key_ref[:, at] = jnp.where(valid, grad_key, 0.0).astype(jnp.bfloat16)
        grad_value_ref[:, at] = jnp.where(valid, grad_value, 0.0).astype(jnp.bfloat16)


def finish_kernel(total_ref, other_ref, starts_ref, out_ref):
    own, _ = starts_of(starts_ref)
    valid = as_column(own) >= 0
    pair = total_ref[...] + other_ref[...].astype(jnp.float32)
    low, high = unpacked(is_heavy(own), pair[:SLOT], pair[SLOT:])
    out_ref[:SLOT, :] = jnp.where(valid[:SLOT], low, 0.0).astype(jnp.bfloat16)
    out_ref[SLOT:, :] = jnp.where(valid[SLOT:], high, 0.0).astype(jnp.bfloat16)


def shards(query_rows, key_rows, value_rows, proj_weight, out_grad, image_starts):
    dp_size, mp_size = lax.axis_size("dp"), lax.axis_size("mp")
    width = query_rows.shape[1]
    near = mp_size // 4
    far = near + 1
    dp, z = lax.axis_index("dp"), lax.axis_index("mp")
    hop_perm = ring_pairs(dp_size, mp_size, 1)
    jump_perm = ring_pairs(dp_size, mp_size, far)
    swap_perm = [(i, (i + dp_size // 2) % dp_size) for i in range(dp_size)]
    right = goes_right(dp, dp_size)
    delta = jnp.where(right, 1, mp_size - 1)
    rows_type = jax.ShapeDtypeStruct((ROWS, width), jnp.bfloat16)
    half_type = jax.ShapeDtypeStruct((ROWS + SLOT, width), jnp.bfloat16)

    def hop(rows):
        return lax.ppermute(rows, ("dp", "mp"), hop_perm)

    def jump(rows):
        return lax.ppermute(rows, ("dp", "mp"), jump_perm)

    def swap(rows):
        return lax.ppermute(rows, "dp", swap_perm)

    def half_of(rows):
        return jnp.where(right, rows[:SLOT], rows[SLOT:])

    def place_half(rows):
        zeros = jnp.zeros_like(rows)
        return jnp.concatenate([jnp.where(right, rows, zeros), jnp.where(right, zeros, rows)], 0)

    def block_of(array, index):
        return lax.dynamic_slice_in_dim(array, lax.rem(index, mp_size) * width, width, 1)

    other_out_grad = swap(out_grad)
    in_any = pl.BlockSpec(memory_space=pl.ANY)
    in_hbm = pl.BlockSpec(memory_space=pltpu.HBM)
    row_buffer = pltpu.VMEM((ROWS, width), jnp.bfloat16)
    attended, own_out_grad, starts = call(
        functools.partial(forward_kernel, dp_size),
        [
            rows_type,
            rows_type,
            jax.ShapeDtypeStruct((2, ROWS), jnp.int32),
        ],
        (query_rows, key_rows, value_rows, out_grad, image_starts),
        specs=[in_hbm] * 5,
        scratch=[row_buffer] * 3
        + [pltpu.VMEM(image_starts.shape, jnp.int32), pltpu.SemaphoreType.DMA((5,))],
        flops=4 * ROWS * ROWS * width,
        name="attention_forward",
        limit=FRONT_LIMIT,
    )
    other_attended = swap(attended)
    (pair_grad,) = call(
        pack_kernel, [rows_type], (own_out_grad, other_out_grad, starts), name="pack_out_grad"
    )
    far_block = jump(pair_grad)
    near_block = hop(pair_grad)
    pair_attended, first_terms = call(
        functools.partial(pack_terms_kernel, dp_size, mp_size, (near, near + far - 1)),
        [rows_type, half_type],
        (attended, other_attended, starts, proj_weight, pair_grad),
        specs=[IN_VMEM] * 4 + [in_any],
        name="pack_attended",
    )

    def product(block, distance):
        return dot(block, block_of(proj_weight, z + distance * (mp_size - delta)), (1, 1))

    def add_terms(sums, step):
        distances = (near - step, near + far - 1 - step)
        joined = jax.ShapeDtypeStruct((2 * ROWS, width), jnp.bfloat16)
        return call(
            functools.partial(add_terms_kernel, dp_size, mp_size, distances),
            [rows_type, rows_type] if step == near - 1 else [joined],
            (sums, pair_attended, proj_weight),
            flops=4 * ROWS * width * width,
            name="add_terms",
        )

    sums = hop(first_terms)
    for step in range(1, near - 1):
        sums = hop(*add_terms(sums, step))
        if step == 1:
            (moved,) = call(
                join_kernel,
                [jax.ShapeDtypeStruct((2 * ROWS, width), jnp.bfloat16)],
                (far_block, near_block, first_terms),
                specs=[IN_VMEM] * 2 + [in_any],
                name="join_out_grad",
            )
    near_sum, last_sum = add_terms(sums, near - 1)
    last_sum, near_sum = jump(last_sum), hop(near_sum)

    partial = place_half(product(half_of(pair_grad), 0))
    for step in range(1, near):
        near_block, far_block = moved[:ROWS], moved[ROWS:]
        partial = partial + product(near_block, step) + product(far_block, far + step - 1)
        if step == near - 1:
            moved = jnp.concatenate([near_block, half_of(far_block)], 0)
        moved = hop(moved)
    near_block, far_block = moved[:ROWS], moved[ROWS:]
    partial = partial + product(near_block, near) + place_half(product(far_block, near + far - 1))
    other_partial = swap(partial.astype(jnp.bfloat16))
    last_sum, other_partial = lax.optimization_barrier((last_sum, other_partial))
    total = (
        near_sum.astype(jnp.float32)
        + last_sum.astype(jnp.float32)
        + place_half(dot(half_of(pair_attended), block_of(proj_weight, z)))
    )
    other_total = swap(total.astype(jnp.bfloat16))
    grads = call(
        backward_kernel,
        [rows_type] * 3,
        (query_rows, key_rows, value_rows, partial, other_partial, starts),
        scratch=[pltpu.VMEM((ROWS, width), jnp.bfloat16)],
        flops=12 * ROWS * ROWS * width,
        name="attention_backward",
    )
    (projected,) = call(
        finish_kernel,
        [rows_type],
        (total, other_total, starts),
        name="finish_projected",
    )
    return (projected, *grads)


def solution(mesh):
    placed = (P("dp", "mp"), P("dp", "mp"), P("dp", "mp"), P("mp", None), P("dp", "mp"), P())
    return jax.shard_map(
        shards,
        mesh=mesh,
        in_specs=placed,
        out_specs=(P("dp", "mp"), P("dp", "mp"), P("dp", "mp"), P("dp", "mp")),
        check_vma=False,
    )
```

```python
import functools
import math

import jax
import jax.numpy as jnp
from jax import lax
from jax.experimental import pallas as pl
from jax.experimental.pallas import tpu as pltpu
from jax.sharding import PartitionSpec as P

HEAD_DIM = 128
SLOT = 128
ROWS = 256
VMEM_LIMIT = 20 * 1024 * 1024
FRONT_LIMIT = 54600 * 1024
IN_VMEM = pl.BlockSpec(memory_space=pltpu.VMEM)


def ring_pairs(dp_size, mp_size, distance):
    pairs = []
    for dp in range(dp_size):
        step = distance if goes_right(dp, dp_size) else mp_size - distance
        for z in range(mp_size):
            pairs.append((dp * mp_size + z, dp * mp_size + (z + step) % mp_size))
    return pairs


def goes_right(dp, dp_size):
    half = dp_size // 2
    if isinstance(dp, int):
        return (dp // half + dp) % 2 == 0
    return lax.rem(lax.div(dp, half) + dp, 2) == 0


def dot(a, b, dims=(1, 0)):
    return lax.dot_general(
        a, b, (((dims[0],), (dims[1],)), ((), ())), preferred_element_type=jnp.float32
    )


def call(kernel, outs, operands, specs=None, scratch=(), flops=0, name=None, limit=VMEM_LIMIT):
    moved = sum(math.prod(a.shape) * a.dtype.itemsize for a in (*operands, *outs))
    return pl.pallas_call(
        kernel,
        out_shape=outs,
        in_specs=specs or [IN_VMEM] * len(operands),
        out_specs=[IN_VMEM] * len(outs),
        scratch_shapes=list(scratch),
        compiler_params=pltpu.CompilerParams(vmem_limit_bytes=limit),
        cost_estimate=pl.CostEstimate(flops=flops, bytes_accessed=moved, transcendentals=0),
        name=name,
    )(*operands)


def starts_of(starts_ref):
    return starts_ref[0:1, :], starts_ref[1:2, :]


def as_column(row):
    size = row.shape[1]
    on_diagonal = lax.broadcasted_iota(jnp.int32, (size, size), 0) == lax.broadcasted_iota(
        jnp.int32, (size, size), 1
    )
    return jnp.sum(jnp.where(on_diagonal, row, 0), axis=1, keepdims=True)


def is_heavy(own):
    lanes = lax.broadcasted_iota(jnp.int32, own.shape, 1)
    return jnp.sum(jnp.where(lanes == SLOT - 1, own, 0)) >= 0


def flip_matrix():
    total = lax.broadcasted_iota(jnp.int32, (SLOT, SLOT), 0) + lax.broadcasted_iota(
        jnp.int32, (SLOT, SLOT), 1
    )
    return jnp.where(total == SLOT - 1, 1.0, 0.0).astype(jnp.bfloat16)


def packed_slots(own_starts, other_starts, own_ref, other_ref):
    heavy = is_heavy(own_starts)
    light_starts = jnp.where(heavy, other_starts, own_starts)
    light_count = jnp.sum((light_starts >= 0).astype(jnp.int32))
    from_light = lax.broadcasted_iota(jnp.int32, (SLOT, 1), 0) < light_count
    own_first, other_first = own_ref[:SLOT, :], other_ref[:SLOT, :]
    first = jnp.where(heavy, own_first, other_first)
    light = jnp.where(heavy, other_first, own_first)
    second = jnp.where(heavy, own_ref[SLOT:, :], other_ref[SLOT:, :])
    flipped = dot(flip_matrix(), second)
    second_slot = jnp.where(from_light, light.astype(jnp.float32), flipped).astype(jnp.bfloat16)
    return first, second_slot


def pack_kernel(own_ref, other_ref, starts_ref, out_ref):
    first, second = packed_slots(*starts_of(starts_ref), own_ref, other_ref)
    out_ref[:SLOT, :] = first
    out_ref[SLOT:, :] = second


def pack_terms_kernel(
    dp_size,
    mp_size,
    distances,
    own_ref,
    other_ref,
    starts_ref,
    weight_ref,
    earlier_ref,
    out_ref,
    terms_ref,
):
    del earlier_ref
    right = goes_right(lax.axis_index("dp"), dp_size)
    first, second = packed_slots(*starts_of(starts_ref), own_ref, other_ref)
    out_ref[:SLOT, :] = first
    out_ref[SLOT:, :] = second
    half = jnp.where(right, first, second)
    near_weight, far_weight = weights_at(dp_size, mp_size, distances, weight_ref)
    terms_ref[:SLOT, :] = dot(first, near_weight).astype(jnp.bfloat16)
    terms_ref[SLOT:ROWS, :] = dot(second, near_weight).astype(jnp.bfloat16)
    terms_ref[ROWS:, :] = dot(half, far_weight).astype(jnp.bfloat16)


def weights_at(dp_size, mp_size, distances, weight_ref):
    width = weight_ref.shape[0]
    right = goes_right(lax.axis_index("dp"), dp_size)
    found = []
    for distance in distances:
        ahead = jnp.where(right, distance, mp_size - distance)
        index = lax.rem(lax.axis_index("mp") + ahead, mp_size)
        found.append(weight_ref[:, pl.ds(pl.multiple_of(index * width, 128), width)])
    return found


def add_terms_kernel(dp_size, mp_size, distances, sums_ref, rows_ref, weight_ref, *out_refs):
    near_weight, far_weight = weights_at(dp_size, mp_size, distances, weight_ref)
    near_term, far_term = dot(rows_ref[...], near_weight), dot(rows_ref[...], far_weight)
    near_sum = sums_ref[:ROWS, :].astype(jnp.float32) + near_term
    if sums_ref.shape[0] == 2 * ROWS:
        far_sum = sums_ref[ROWS:, :].astype(jnp.float32) + far_term
    else:
        right = goes_right(lax.axis_index("dp"), dp_size)
        half = sums_ref[ROWS:, :].astype(jnp.float32)
        first = jnp.where(right, half, 0.0) + far_term[:SLOT]
        second = jnp.where(right, 0.0, half) + far_term[SLOT:]
        far_sum = jnp.concatenate([first, second], 0)
    if len(out_refs) == 2:
        out_refs[0][...] = near_sum.astype(jnp.bfloat16)
        out_refs[1][...] = far_sum.astype(jnp.bfloat16)
    else:
        out_refs[0][:ROWS, :] = near_sum.astype(jnp.bfloat16)
        out_refs[0][ROWS:, :] = far_sum.astype(jnp.bfloat16)


def total_kernel(
    dp_size,
    mp_size,
    last_ref,
    near_ref,
    rows_ref,
    weight_ref,
    earlier_ref,
    total_ref,
    sent_ref,
):
    del earlier_ref
    right = goes_right(lax.axis_index("dp"), dp_size)
    (weight,) = weights_at(dp_size, mp_size, (0,), weight_ref)
    own = dot(jnp.where(right, rows_ref[:SLOT, :], rows_ref[SLOT:, :]), weight)
    total = near_ref[...].astype(jnp.float32) + last_ref[...].astype(jnp.float32)
    total_ref[:SLOT, :] = total[:SLOT] + jnp.where(right, own, 0.0)
    total_ref[SLOT:, :] = total[SLOT:] + jnp.where(right, 0.0, own)
    sent_ref[...] = total_ref[...].astype(jnp.bfloat16)


def join_kernel(far_ref, near_ref, earlier_ref, out_ref):
    del earlier_ref
    out_ref[:ROWS, :] = near_ref[...]
    out_ref[ROWS:, :] = far_ref[...]


def probabilities_of(query, key, same_image):
    scores = dot(query, key, (1, 1)) / math.sqrt(HEAD_DIM)
    scores = jnp.where(same_image, scores, -jnp.inf)
    weights = jnp.exp(scores - jnp.max(scores, axis=1, keepdims=True))
    return weights * (1.0 / jnp.sum(weights, axis=1, keepdims=True))


def forward_kernel(
    dp_size,
    query_hbm,
    key_hbm,
    value_hbm,
    out_grad_hbm,
    starts_hbm,
    out_ref,
    out_grad_ref,
    pair_starts_ref,
    query_ref,
    key_ref,
    value_ref,
    starts_ref,
    sems,
):
    width = query_ref.shape[1]
    dp = lax.axis_index("dp")
    moves = [
        (starts_hbm, starts_ref),
        (query_hbm, query_ref),
        (key_hbm, key_ref),
        (value_hbm, value_ref),
        (out_grad_hbm, out_grad_ref),
    ]
    copies = [pltpu.make_async_copy(*move, sems.at[at]) for at, move in enumerate(moves)]
    for copy in copies:
        copy.start()
    copies[0].wait()
    own = starts_ref[pl.ds(dp, 1), :]
    pair_starts_ref[0:1, :] = own
    pair_starts_ref[1:2, :] = starts_ref[pl.ds(lax.rem(dp + dp_size // 2, dp_size), 1), :]
    for copy in copies[1:4]:
        copy.wait()
    same_image = as_column(own) == own
    for head in range(width // HEAD_DIM):
        at = slice(head * HEAD_DIM, (head + 1) * HEAD_DIM)
        rounded = probabilities_of(query_ref[:, at], key_ref[:, at], same_image).astype(jnp.bfloat16)
        out_ref[:, at] = dot(rounded, value_ref[:, at]).astype(jnp.bfloat16)
    for copy in copies[4:]:
        copy.wait()


def unpacked(heavy, first, second):
    own_first = jnp.where(heavy, first, second)
    return own_first, dot(flip_matrix(), second.astype(jnp.bfloat16))


def backward_kernel(
    query_ref,
    key_ref,
    value_ref,
    partial_ref,
    other_ref,
    starts_ref,
    grad_query_ref,
    grad_key_ref,
    grad_value_ref,
    grad_ref,
):
    own, _ = starts_of(starts_ref)
    column = as_column(own)
    same_image = column == own
    valid = column >= 0
    pair = partial_ref[...] + other_ref[...].astype(jnp.float32)
    low, high = unpacked(is_heavy(own), pair[:SLOT], pair[SLOT:])
    grad_ref[:SLOT, :] = low.astype(jnp.bfloat16)
    grad_ref[SLOT:, :] = high.astype(jnp.bfloat16)
    for head in range(query_ref.shape[1] // HEAD_DIM):
        at = slice(head * HEAD_DIM, (head + 1) * HEAD_DIM)
        query, key, value, grad = query_ref[:, at], key_ref[:, at], value_ref[:, at], grad_ref[:, at]
        probabilities = probabilities_of(query, key, same_image)
        rounded = probabilities.astype(jnp.bfloat16)
        grad_value = dot(rounded, grad, (0, 0))
        grad_weights = dot(grad, value, (1, 1))
        correction = jnp.sum(probabilities * grad_weights, axis=1, keepdims=True)
        grad_scores = (probabilities * (grad_weights - correction) / math.sqrt(HEAD_DIM)).astype(
            jnp.bfloat16
        )
        grad_query = dot(grad_scores, key)
        grad_key = dot(grad_scores, query, (0, 0))
        grad_query_ref[:, at] = jnp.where(valid, grad_query, 0.0).astype(jnp.bfloat16)
        grad_key_ref[:, at] = jnp.where(valid, grad_key, 0.0).astype(jnp.bfloat16)
        grad_value_ref[:, at] = jnp.where(valid, grad_value, 0.0).astype(jnp.bfloat16)


def finish_kernel(total_ref, other_ref, starts_ref, out_ref):
    own, _ = starts_of(starts_ref)
    valid = as_column(own) >= 0
    pair = total_ref[...] + other_ref[...].astype(jnp.float32)
    low, high = unpacked(is_heavy(own), pair[:SLOT], pair[SLOT:])
    out_ref[:SLOT, :] = jnp.where(valid[:SLOT], low, 0.0).astype(jnp.bfloat16)
    out_ref[SLOT:, :] = jnp.where(valid[SLOT:], high, 0.0).astype(jnp.bfloat16)


def shards(query_rows, key_rows, value_rows, proj_weight, out_grad, image_starts):
    dp_size, mp_size = lax.axis_size("dp"), lax.axis_size("mp")
    width = query_rows.shape[1]
    near = mp_size // 4
    far = near + 1
    dp, z = lax.axis_index("dp"), lax.axis_index("mp")
    hop_perm = ring_pairs(dp_size, mp_size, 1)
    jump_perm = ring_pairs(dp_size, mp_size, far)
    swap_perm = [(i, (i + dp_size // 2) % dp_size) for i in range(dp_size)]
    right = goes_right(dp, dp_size)
    delta = jnp.where(right, 1, mp_size - 1)
    rows_type = jax.ShapeDtypeStruct((ROWS, width), jnp.bfloat16)
    half_type = jax.ShapeDtypeStruct((ROWS + SLOT, width), jnp.bfloat16)

    def hop(rows):
        return lax.ppermute(rows, ("dp", "mp"), hop_perm)

    def jump(rows):
        return lax.ppermute(rows, ("dp", "mp"), jump_perm)

    def swap(rows):
        return lax.ppermute(rows, "dp", swap_perm)

    def half_of(rows):
        return jnp.where(right, rows[:SLOT], rows[SLOT:])

    def place_half(rows):
        zeros = jnp.zeros_like(rows)
        return jnp.concatenate([jnp.where(right, rows, zeros), jnp.where(right, zeros, rows)], 0)

    def block_of(array, index):
        return lax.dynamic_slice_in_dim(array, lax.rem(index, mp_size) * width, width, 1)

    other_out_grad = swap(out_grad)
    in_any = pl.BlockSpec(memory_space=pl.ANY)
    in_hbm = pl.BlockSpec(memory_space=pltpu.HBM)
    row_buffer = pltpu.VMEM((ROWS, width), jnp.bfloat16)
    attended, own_out_grad, starts = call(
        functools.partial(forward_kernel, dp_size),
        [
            rows_type,
            rows_type,
            jax.ShapeDtypeStruct((2, ROWS), jnp.int32),
        ],
        (query_rows, key_rows, value_rows, out_grad, image_starts),
        specs=[in_hbm] * 5,
        scratch=[row_buffer] * 3
        + [pltpu.VMEM(image_starts.shape, jnp.int32), pltpu.SemaphoreType.DMA((5,))],
        flops=4 * ROWS * ROWS * width,
        name="attention_forward",
        limit=FRONT_LIMIT,
    )
    other_attended = swap(attended)
    (pair_grad,) = call(
        pack_kernel, [rows_type], (own_out_grad, other_out_grad, starts), name="pack_out_grad"
    )
    far_block = jump(pair_grad)
    near_block = hop(pair_grad)
    pair_attended, first_terms = call(
        functools.partial(pack_terms_kernel, dp_size, mp_size, (near, near + far - 1)),
        [rows_type, half_type],
        (attended, other_attended, starts, proj_weight, pair_grad),
        specs=[IN_VMEM] * 4 + [in_any],
        name="pack_attended",
    )

    def product(block, distance):
        return dot(block, block_of(proj_weight, z + distance * (mp_size - delta)), (1, 1))

    def add_terms(sums, step):
        distances = (near - step, near + far - 1 - step)
        joined = jax.ShapeDtypeStruct((2 * ROWS, width), jnp.bfloat16)
        return call(
            functools.partial(add_terms_kernel, dp_size, mp_size, distances),
            [rows_type, rows_type] if step == near - 1 else [joined],
            (sums, pair_attended, proj_weight),
            flops=4 * ROWS * width * width,
            name="add_terms",
        )

    sums = hop(first_terms)
    for step in range(1, near - 1):
        sums = hop(*add_terms(sums, step))
        if step == 1:
            (moved,) = call(
                join_kernel,
                [jax.ShapeDtypeStruct((2 * ROWS, width), jnp.bfloat16)],
                (far_block, near_block, first_terms),
                specs=[IN_VMEM] * 2 + [in_any],
                name="join_out_grad",
            )
    near_sum, last_sum = add_terms(sums, near - 1)
    last_sum, near_sum = jump(last_sum), hop(near_sum)

    partial = place_half(product(half_of(pair_grad), 0))
    for step in range(1, near):
        near_block, far_block = moved[:ROWS], moved[ROWS:]
        partial = partial + product(near_block, step) + product(far_block, far + step - 1)
        if step == near - 1:
            moved = jnp.concatenate([near_block, half_of(far_block)], 0)
        moved = hop(moved)
    near_block, far_block = moved[:ROWS], moved[ROWS:]
    partial = partial + product(near_block, near) + place_half(product(far_block, near + far - 1))
    other_partial = swap(partial.astype(jnp.bfloat16))
    total, sent = call(
        functools.partial(total_kernel, dp_size, mp_size),
        [jax.ShapeDtypeStruct((ROWS, width), jnp.float32), rows_type],
        (last_sum, near_sum, pair_attended, proj_weight, partial),
        specs=[IN_VMEM] * 4 + [in_any],
        flops=2 * SLOT * width * width,
        name="total",
    )
    other_total = swap(sent)
    grads = call(
        backward_kernel,
        [rows_type] * 3,
        (query_rows, key_rows, value_rows, partial, other_partial, starts),
        scratch=[pltpu.VMEM((ROWS, width), jnp.bfloat16)],
        flops=12 * ROWS * ROWS * width,
        name="attention_backward",
    )
    (projected,) = call(
        finish_kernel,
        [rows_type],
        (total, other_total, starts),
        name="finish_projected",
    )
    return (projected, *grads)


def solution(mesh):
    placed = (P("dp", "mp"), P("dp", "mp"), P("dp", "mp"), P("mp", None), P("dp", "mp"), P())
    return jax.shard_map(
        shards,
        mesh=mesh,
        in_specs=placed,
        out_specs=(P("dp", "mp"), P("dp", "mp"), P("dp", "mp"), P("dp", "mp")),
        check_vma=False,
    )
```
